128 devices in a mesh: dp: 4 (over z_lo, core), fsdp: 32 (over z_hi, x, y).
Axes of the slice: x: 4, y: 4, z: 4 (z_hi: 2, z_lo: 2; z = z_hi * 2 + z_lo), core: 2. Of those that a mesh axis runs over, the one named last changes fastest.
Arguments:
- feat_s: bfloat16 [16384, 6144], P(('dp', 'fsdp')), may hold values from -6 to 6
- feat_t: bfloat16 [16384, 6144], P(('dp', 'fsdp')), may hold values from -6 to 6
- bot_s: float32 [6144, 256], P(('dp', 'fsdp')), may hold values from -0.078125 to 0.078125
- bot_m: float32 [6144, 256], P(('dp', 'fsdp')), may hold values from -0.006 to 0.006
- bot_v: float32 [6144, 256], P(('dp', 'fsdp')), may hold values from 1e-07 to 1e-05
- bot_t: float32 [6144, 256], P(('dp', 'fsdp')), may hold values from -0.078125 to 0.078125
- proto_s: float32 [256, 32768], P(None, ('fsdp', 'dp')), may hold values from -0.1 to 0.1
- proto_m: float32 [256, 32768], P(None, ('fsdp', 'dp')), may hold values from -0.006 to 0.006
- proto_v: float32 [256, 32768], P(None, ('fsdp', 'dp')), may hold values from 1e-07 to 1e-05
- proto_t: float32 [256, 32768], P(None, ('fsdp', 'dp')), may hold values from -0.1 to 0.1
Outputs:
- new_bot_s: float32 [6144, 256], P(('dp', 'fsdp'))
- new_bot_m: float32 [6144, 256], P(('dp', 'fsdp'))
- new_bot_v: float32 [6144, 256], P(('dp', 'fsdp'))
- new_bot_t: float32 [6144, 256], P(('dp', 'fsdp'))
- new_proto_s: float32 [256, 32768], P(None, ('fsdp', 'dp'))
- new_proto_m: float32 [256, 32768], P(None, ('fsdp', 'dp'))
- new_proto_v: float32 [256, 32768], P(None, ('fsdp', 'dp'))
- new_proto_t: float32 [256, 32768], P(None, ('fsdp', 'dp'))
The draws below stay inside these ranges and needn't reach their ends.
All inputs are finite; a program needn't handle non-finite values.
Results may differ from the reference program's by a relative error of at most 0.0045.
The reference program's roundings to bfloat16 on the way (of `dz` and `dy`) count: a program that leaves them out, or rounds other values in their place, can miss the bound.
Values may be sent and summed in bfloat16 or wider, within the bound.
A program may use at most 128 MiB of HBM per device.

```python
import math
import jax
import jax.numpy as jnp
from jax import lax

D = 6144
BOT = 256
PROTOS = 32768
TOKENS = 16384


def levels(own_key, dims, cuts, least, high):
    gain, own = 1.0, jax.random.fold_in(own_key, 6)
    for axis_at, blocks in cuts:
        draws = jnp.exp(jax.random.uniform(jax.random.fold_in(own, axis_at), (blocks,), jnp.float32, least / len(cuts), high / len(cuts)))
        gain = gain * jnp.repeat(draws, dims[axis_at] // blocks).reshape([-1 if axis == axis_at else 1 for axis in range(len(dims))])
    return gain


def centred(stream_key, dims, width, most, cuts=(), dtype=jnp.bfloat16):
    array = jax.random.normal(stream_key, dims, jnp.float32) * width
    if len(cuts) > 0:
        array = levels(stream_key, dims, cuts, -0.22, 0.18) * array
    return jnp.clip(array, min=-most, max=most).astype(dtype)


def setup_inputs(seed: int = 0) -> dict:
    key_list = jax.random.split(jax.random.key(seed), 11)
    feat_s = centred(key_list[0], (TOKENS, D), 1.0, 6.0, ((0, 128),))
    feat_t = centred(key_list[1], (TOKENS, D), 1.0, 6.0, ((0, 128),))
    bot_s = centred(key_list[2], (D, BOT), D ** -0.5, 0.078125, ((0, 128),), jnp.float32)
    bot_m = centred(key_list[3], (D, BOT), 0.001, 0.006, ((0, 128),), jnp.float32)
    bot_v = jnp.clip(jnp.exp(math.log(9.999999747378752e-06) - 4.6051701 * jax.random.uniform(key_list[4], (D, BOT), jnp.float32) ** levels(key_list[4], (D, BOT), ((0, 128),), -0.2, 0.2)), 1.0000000116860974e-07, 9.999999747378752e-06)
    bot_t = centred(key_list[5], (D, BOT), D ** -0.5, 0.078125, ((0, 128),), jnp.float32)
    proto_s = jnp.clip(jax.random.uniform(key_list[6], (BOT, PROTOS), jnp.float32, -0.1, 0.1) * levels(key_list[6], (BOT, PROTOS), ((1, 128),), -0.4, 0.0), -0.1, 0.1)
    proto_m = centred(key_list[7], (BOT, PROTOS), 0.001, 0.006, ((1, 128),), jnp.float32)
    proto_v = jnp.clip(jnp.exp(math.log(9.999999747378752e-06) - 4.6051701 * jax.random.uniform(key_list[8], (BOT, PROTOS), jnp.float32) ** levels(key_list[8], (BOT, PROTOS), ((1, 128),), -0.2, 0.2)), 1.0000000116860974e-07, 9.999999747378752e-06)
    proto_t = jnp.clip(jax.random.uniform(key_list[9], (BOT, PROTOS), jnp.float32, -0.1, 0.1) * levels(key_list[9], (BOT, PROTOS), ((1, 128),), -0.4, 0.0), -0.1, 0.1)
    return dict(feat_s=feat_s, feat_t=feat_t, bot_s=bot_s, bot_m=bot_m, bot_v=bot_v, bot_t=bot_t, proto_s=proto_s, proto_m=proto_m, proto_v=proto_v, proto_t=proto_t)


tau_student = 0.1
tau_teacher = 0.04
bias_first = 0.99997343860111
bias_second = 0.0952078527

def adamw(param, first, second, grad, teacher):
    first_new = 0.9 * first + 0.1 * grad
    second_new = 0.999 * second + 0.001 * grad * grad
    direction = first_new / bias_first / (jnp.sqrt(second_new / bias_second) + 1e-08)
    param_new = param - 0.002 * (direction + 0.04 * param)
    teacher_new = 0.996 * teacher + 0.004 * param_new
    return (param_new, first_new, second_new, teacher_new)

def reference(feat_s, feat_t, bot_s, bot_m, bot_v, bot_t, proto_s, proto_m, proto_v, proto_t):
    bs = bot_s.astype(jnp.bfloat16)
    bt = bot_t.astype(jnp.bfloat16)
    ps = proto_s.astype(jnp.bfloat16)
    pt = proto_t.astype(jnp.bfloat16)
    ys = jnp.dot(feat_s, bs, preferred_element_type=jnp.float32)
    yt = jnp.dot(feat_t, bt, preferred_element_type=jnp.float32)
    norm_s = jnp.sqrt(lax.optimization_barrier(jnp.sum(ys * ys, axis=1, keepdims=True)) + 1e-06)
    norm_t = jnp.sqrt(lax.optimization_barrier(jnp.sum(yt * yt, axis=1, keepdims=True)) + 1e-06)
    unit_s = ys / norm_s
    codes_s = unit_s.astype(jnp.bfloat16)
    codes_t = (yt / norm_t).astype(jnp.bfloat16)
    block = math.gcd(TOKENS, 512)
    count = TOKENS // block

    def step(carry, pair):
        cs, ct = pair
        es = jnp.exp(jnp.dot(cs, ps, preferred_element_type=jnp.float32) / tau_student)
        et = jnp.exp(jnp.dot(ct, pt, preferred_element_type=jnp.float32) / tau_teacher)
        qs = es / lax.optimization_barrier(jnp.sum(es, axis=1, keepdims=True))
        qt = et / lax.optimization_barrier(jnp.sum(et, axis=1, keepdims=True))
        dz = ((qs - qt) / tau_student).astype(jnp.bfloat16)
        carry = carry + lax.dot_general(cs, dz, (((0,), (0,)), ((), ())), preferred_element_type=jnp.float32)
        dh = lax.dot_general(dz, ps, (((1,), (1,)), ((), ())), preferred_element_type=jnp.float32)
        return (carry, dh)
    start = jnp.zeros((BOT, PROTOS), jnp.float32)
    g_proto, dh_blocks = lax.scan(step, start, (codes_s.reshape(count, block, BOT), codes_t.reshape(count, block, BOT)))
    dh = dh_blocks.reshape(TOKENS, BOT)
    dy = ((dh - unit_s * lax.optimization_barrier(jnp.sum(unit_s * dh, axis=1, keepdims=True))) / norm_s).astype(jnp.bfloat16)
    g_bot = lax.dot_general(feat_s, dy, (((0,), (0,)), ((), ())), preferred_element_type=jnp.float32)
    b_s, b_m, b_v, b_t = adamw(bot_s, bot_m, bot_v, g_bot, bot_t)
    p_s, p_m, p_v, p_t = adamw(proto_s, proto_m, proto_v, g_proto, proto_t)
    return (b_s, b_m, b_v, b_t, p_s, p_m, p_v, p_t)
```

```python
import math

import jax
import jax.numpy as jnp
from jax import lax
from jax.experimental import pallas as pl
from jax.experimental.pallas import tpu as pltpu
from jax.sharding import PartitionSpec as P

MESH = pl.DeviceIdType.MESH
F32, BF16 = jnp.float32, jnp.bfloat16
tau_student = 0.1
tau_teacher = 0.04
bias_first = 0.99997343860111
bias_second = 0.0952078527
LOG2E = math.log2(math.e)
PB = 256
NB = 8
NP = PB * NB
TB = 128
NT = 16 * TB
PC = 512
SEMS = 112


def adamw(param, first, second, grad, teacher):
    first_new = 0.9 * first + 0.1 * grad
    second_new = 0.999 * second + 0.001 * grad * grad
    direction = first_new / bias_first / (jnp.sqrt(second_new / bias_second) + 1e-08)
    param_new = param - 0.002 * (direction + 0.04 * param)
    teacher_new = 0.996 * teacher + 0.004 * param_new
    return (param_new, first_new, second_new, teacher_new)


def run(*steps):
    steps = list(steps)
    while steps:
        for step in list(steps):
            try:
                next(step)
            except StopIteration:
                steps.remove(step)


def dot(a, b, dims=((1,), (0,))):
    return lax.dot_general(a, b, (dims, ((), ())), preferred_element_type=F32)


def kernel(
    feat_s, feat_t, bot_s, bot_t, proto_s, proto_t,
    g_bot, g_proto,
    w, fx, yf, yr, unit, norm, cs, ct, ps, pt, pn, es, et, dz,
    tx, ty, tot, dh0, dhr0, dh1, dhr1, grecv, gz, gzr,
    dy, b0, br0, b1, br1, b2, br2,
    send_sem, recv_sem, local_sem,
):
    dp, fs = lax.axis_index("dp"), lax.axis_index("fsdp")
    core, zl = lax.rem(dp, 2), lax.div(dp, 2)
    zh, x, y = lax.div(fs, 16), lax.rem(lax.div(fs, 4), 4), lax.rem(fs, 4)
    z = zh * 2 + zl
    other = 1 - core
    turn = 1 + 2 * core

    def device(x=x, y=y, z=z, core=core):
        return {"dp": lax.rem(z, 2) * 2 + core, "fsdp": lax.div(z, 2) * 16 + x * 4 + y}

    place = {"x": x, "y": y, "z": z}

    def ring(axis):
        at = place[axis]
        ahead, behind = lax.rem(at + turn, 4), lax.rem(at + 4 - turn, 4)
        return at, ahead, behind, lax.rem(at + 2, 4)

    copies = []

    def push(src, dst, to):
        at = len(copies)
        copy = pltpu.make_async_remote_copy(
            src_ref=src, dst_ref=dst, send_sem=send_sem.at[at], recv_sem=recv_sem.at[at],
            device_id=to, device_id_type=MESH,
        )
        copy.start()
        copies.append(copy)
        return copy

    def gather(axis, block):
        at, ahead, behind, _ = ring(axis)
        up = push(block(at), block(at), device(**{axis: ahead}))
        down = push(block(at), block(at), device(**{axis: behind}))
        yield
        up.wait_recv()
        on = push(block(behind), block(behind), device(**{axis: ahead}))
        yield
        down.wait_recv()
        on.wait_recv()

    def scatter(axis, parts, recv, put):
        at, ahead, behind, far = ring(axis)
        up = push(parts.at[far], recv.at[0], device(**{axis: ahead}))
        down = push(parts.at[behind], recv.at[1], device(**{axis: behind}))
        yield
        up.wait_recv()
        parts[ahead] = (parts[ahead].astype(F32) + recv[0].astype(F32)).astype(parts.dtype)
        on = push(parts.at[ahead], recv.at[2], device(**{axis: ahead}))
        yield
        down.wait_recv()
        total = parts[at].astype(F32) + recv[1].astype(F32)
        on.wait_recv()
        put(total + recv[2].astype(F32))

    barrier = pltpu.get_barrier_semaphore()
    peers = [device(core=other)]
    for axis in ("x", "y", "z"):
        for step in (1, 3) if axis == "z" else (1, 2, 3):
            peers.append(device(**{axis: lax.rem(place[axis] + step, 4)}))
    for peer in peers:
        pl.semaphore_signal(barrier, inc=1, device_id=peer, device_id_type=MESH)

    local = []
    for side, feat in enumerate((feat_s, feat_t)):
        for half in range(2):
            columns = pl.ds(pl.multiple_of((half * 2 + core) * 1536, 1536), 1536)
            rows = pl.ds(pl.multiple_of(core * TB, TB), TB)
            copy = pltpu.make_async_copy(
                feat.at[:, columns], fx.at[side, half, rows, :], local_sem.at[side * 2 + half]
            )
            copy.start()
            local.append(copy)
    w[zl, zh, x, y, :, 0:256] = bot_s[...].astype(BF16)
    w[zl, zh, x, y, :, 256:512] = bot_t[...].astype(BF16)
    pl.semaphore_wait(barrier, len(peers))

    def part(k):
        return pl.ds(16 * k, 16)

    def bot_gather(k):
        r = part(k)
        if k == 0:
            yield from gather("x", lambda c: w.at[zl, zh, c, y, r, :])
            yield from gather("y", lambda c: w.at[zl, zh, :, c, r, :])
            yield from gather("z", lambda c: w.at[lax.rem(c, 2), lax.div(c, 2), :, :, r, :])
        elif k == 1:
            yield from gather("y", lambda c: w.at[zl, zh, x, c, r, :])
            yield from gather("z", lambda c: w.at[lax.rem(c, 2), lax.div(c, 2), x, :, r, :])
            yield from gather("x", lambda c: w.at[:, :, c, :, r, :])
        else:
            yield from gather("z", lambda c: w.at[lax.rem(c, 2), lax.div(c, 2), x, y, r, :])
            yield from gather("x", lambda c: w.at[:, :, c, y, r, :])
            yield from gather("y", lambda c: w.at[:, :, :, c, r, :])

    def features():
        got = []
        for side, feat in enumerate((feat_s, feat_t)):
            for half in range(2):
                columns = pl.ds(pl.multiple_of((half * 2 + other) * 1536, 1536), 1536)
                rows = pl.ds(pl.multiple_of(core * TB, TB), TB)
                got.append(push(feat.at[:, columns], fx.at[side, half, rows, :], device(core=other)))
        ps[z, core] = proto_s[...].T.astype(BF16)
        pt[z, core] = proto_t[...].T.astype(BF16)
        yield
        yield
        for copy in got:
            copy.wait_recv()
        for copy in local:
            copy.wait()

    run(bot_gather(0), bot_gather(1), bot_gather(2), features())
    gathered = list(copies)

    proto_steps = [gather("z", lambda c: ps.at[c, core]), gather("z", lambda c: pt.at[c, core])]
    for step in proto_steps:
        next(step)

    for side in range(2):
        total = jnp.zeros((2 * TB, 256), F32)
        for a in range(2):
            for b in range(2):
                block = w[a, b, :, :, :, pl.ds(256 * side, 256)].reshape(768, 256)
                total += dot(fx[side, a, :, pl.ds(768 * b, 768)], block)
        yf[side, 0] = total[:TB]
        yf[side, 1] = total[TB:]
    swap = push(yf.at[:, other], yr, device(core=other))
    for step in proto_steps:
        next(step)
    swap.wait_recv()
    for side in range(2):
        yt = (yf[side, core] + yr[side]).T
        n = jnp.sqrt(jnp.sum(yt * yt, axis=0, keepdims=True) + 1e-06)
        u = yt / n
        if side == 0:
            unit[...] = u
            norm[0:1, :] = n
        (cs, ct)[side][x, y] = u.T.astype(BF16)

    def codes(side):
        if side == 0:
            yield from gather("x", lambda c: cs.at[c, y])
            yield from gather("y", lambda c: cs.at[:, c])
        else:
            yield from gather("y", lambda c: ct.at[x, c])
            yield from gather("x", lambda c: ct.at[c])

    def transposed():
        for copy in gathered:
            copy.wait_send()
        for a in range(2):
            for b in range(2):
                block = fx[0, a, :, pl.ds(768 * b, 768)].T
                w[a, b, :, :, :, 0:256] = block.reshape(4, 4, 48, 256)
        yield

    def protos():
        yield
        for step in proto_steps:
            run(step)
        swaps = [push(ref.at[:, core], ref.at[:, core], device(core=other)) for ref in (ps, pt)]
        yield
        yield
        for copy in swaps:
            copy.wait_recv()
        for b in range(NB):
            pn[:, b * PB : (b + 1) * PB] = ps[b // 2, b % 2].T

    run(codes(0), codes(1), transposed(), protos())

    blocks = PC // PB
    for side, (code, proto, out, scale) in enumerate(
        ((cs, ps, es, LOG2E / tau_student), (ct, pt, et, LOG2E / tau_teacher))
    ):

        def tokens(i, _, side=side, code=code, proto=proto, out=out, scale=scale):
            a, b = lax.div(i, 2), lax.rem(i, 2) * 2
            c = code[a, pl.ds(b, 2)].reshape(2 * TB, 256)

            def some(j, total):
                p = proto[j].reshape(PC, 256)
                e = jnp.exp2(dot(p, c, ((1,), (1,))) * scale)
                out[i, pl.ds(pl.multiple_of(j * PC, PC), PC), :] = e
                return total + jnp.sum(e.reshape(PC // 8, 8, 2 * TB), axis=0)

            total = lax.fori_loop(0, NP // PC, some, jnp.zeros((8, 2 * TB), F32))
            total = jnp.sum(total, axis=0, keepdims=True)
            tx[x, side, pl.ds(i * 2, 1), :] = total[:, :TB]
            tx[x, side, pl.ds(i * 2 + 1, 1), :] = total[:, TB:]
            return 0

        lax.fori_loop(0, NT // (2 * TB), tokens, 0)

    sent = [push(tx.at[x], tx.at[x], device(x=lax.rem(x + d, 4))) for d in (1, 2, 3)]
    for copy in sent:
        copy.wait_recv()
    ty[y] = tx[0] + tx[1] + tx[2] + tx[3]
    sent = [push(ty.at[y], ty.at[y], device(y=lax.rem(y + d, 4))) for d in (1, 2, 3)]
    for copy in sent:
        copy.wait_recv()
    tot[...] = (1.0 / tau_student) / (ty[0] + ty[1] + ty[2] + ty[3])

    def back(i, _):
        inv_s = jnp.concatenate([tot[0, pl.ds(2 * i, 1), :], tot[0, pl.ds(2 * i + 1, 1), :]], 1)
        inv_t = jnp.concatenate([tot[1, pl.ds(2 * i, 1), :], tot[1, pl.ds(2 * i + 1, 1), :]], 1)
        columns = pl.ds(pl.multiple_of(i * 2 * TB, 2 * TB), 2 * TB)

        def some(j, _):
            rows = pl.ds(pl.multiple_of(j * PC, PC), PC)
            dz[rows, columns] = (es[i, rows, :] * inv_s - et[i, rows, :] * inv_t).astype(BF16)
            return 0

        lax.fori_loop(0, NP // PC, some, 0)
        dh = dot(pn[...], dz[:, columns])
        a, b = lax.div(i, 2), lax.rem(i, 2) * 2
        for d in range(2):
            dh0[0, a, b + d] = dh[:128, d * TB : (d + 1) * TB].astype(BF16)
            dh0[1, b + d, a] = dh[128:, d * TB : (d + 1) * TB].astype(BF16)
        return 0

    lax.fori_loop(0, NT // (2 * TB), back, 0)

    def dh_scatter(k):
        def middle(v):
            dh1[k] = v

        def last(v):
            dhr1[k, 0] = v

        yield from scatter("xy"[k], dh0.at[k], dhr0.at[k], middle)
        yield from scatter("yx"[k], dh1.at[k], dhr1.at[k], last)

    def proto_grad():
        def grad(block):
            rows = pl.ds(pl.multiple_of(block * PB, PB), PB)
            return dot(dz[rows, :], cs[...].reshape(NT, 256))

        def theirs(i, _):
            es[0, pl.ds(pl.multiple_of(i * PB, PB), PB), :] = grad(i * 2 + other)
            return 0

        def ours(i, _):
            es[1, pl.ds(pl.multiple_of(i * PB, PB), PB), :] = grad(i * 2 + core)
            return 0

        lax.fori_loop(0, 4, theirs, 0)
        swap = push(es.at[0, pl.ds(0, 4 * PB), :], grecv, device(core=other))
        yield
        lax.fori_loop(0, 4, ours, 0)
        swap.wait_recv()
        gz[...] = (es[1, : 4 * PB, :] + grecv[...]).astype(BF16).reshape(4, PB, 256)

        def last(v):
            g_proto[...] = v.T

        yield from scatter("z", gz, gzr, last)

    proto_steps = proto_grad()
    run(dh_scatter(0), dh_scatter(1), proto_steps)

    dht = jnp.concatenate([dhr1[0, 0], dhr1[1, 0]], axis=0)
    u = unit[...]
    dyt = (dht - u * jnp.sum(u * dht, axis=0, keepdims=True)) / norm[0:1, :]
    dy[core] = dyt.astype(BF16)
    swap = push(dy.at[core], dy.at[core], device(core=other))
    swap.wait_recv()

    dyb = jnp.concatenate([dy[0], dy[1]], axis=1)
    for a in range(2):
        for b in range(2):
            c = b * 2 + a
            g = dot(w[a, b, :, :, :, 0:256].reshape(768, 256), dyb, ((1,), (1,))).astype(BF16)
            g = g.reshape(4, 4, 48, 256)
            for i in range(4):
                for j in range(4):
                    b0[0, i, j, c] = g[i, j, 0:16]
                    b0[1, j, c, i] = g[i, j, 16:32]
                    b0[2, c, i, j] = g[i, j, 32:48]

    def bot_scatter(k):
        def first(v):
            b1[k] = v

        def second(v):
            b2[k] = v

        def last(v):
            g_bot[16 * k : 16 * (k + 1), :] = v

        one, two, three = ("xyz", "yzx", "zxy")[k]
        yield from scatter(one, b0.at[k], br0.at[k], first)
        yield from scatter(two, b1.at[k], br1.at[k], second)
        yield from scatter(three, b2.at[k], br2.at[k], last)

    run(bot_scatter(0), bot_scatter(1), bot_scatter(2))
    for copy in copies[len(gathered) :]:
        copy.wait_send()


def gradients(feat_s, feat_t, bot_s, bot_t, proto_s, proto_t):
    whole = pl.BlockSpec(memory_space=pltpu.VMEM)
    vmem = pltpu.VMEM
    return pl.pallas_call(
        kernel,
        out_shape=(
            jax.ShapeDtypeStruct((48, 256), F32),
            jax.ShapeDtypeStruct((256, PB), F32),
        ),
        in_specs=[pl.BlockSpec(memory_space=pl.ANY)] * 2 + [whole] * 4,
        out_specs=(whole, whole),
        scratch_shapes=[
            vmem((2, 2, 4, 4, 48, 512), BF16),
            vmem((2, 2, 2 * TB, 1536), BF16),
            vmem((2, 2, TB, 256), F32),
            vmem((2, TB, 256), F32),
            vmem((256, TB), F32),
            vmem((8, TB), F32),
            vmem((4, 4, TB, 256), BF16),
            vmem((4, 4, TB, 256), BF16),
            vmem((4, 2, PB, 256), BF16),
            vmem((4, 2, PB, 256), BF16),
            vmem((256, NP), BF16),
            vmem((8, NP, 2 * TB), F32),
            vmem((8, NP, 2 * TB), F32),
            vmem((NP, NT), BF16),
            vmem((4, 2, 16, TB), F32),
            vmem((4, 2, 16, TB), F32),
            vmem((2, 16, TB), F32),
            vmem((2, 4, 4, 128, TB), BF16),
            vmem((2, 3, 4, 128, TB), BF16),
            vmem((2, 4, 128, TB), F32),
            vmem((2, 3, 128, TB), F32),
            vmem((4 * PB, 256), F32),
            vmem((4, PB, 256), BF16),
            vmem((3, PB, 256), BF16),
            vmem((2, 256, TB), BF16),
            vmem((3, 4, 4, 4, 16, 256), BF16),
            vmem((3, 3, 4, 4, 16, 256), BF16),
            vmem((3, 4, 4, 16, 256), F32),
            vmem((3, 3, 4, 16, 256), F32),
            vmem((3, 4, 16, 256), F32),
            vmem((3, 3, 16, 256), F32),
            pltpu.SemaphoreType.DMA((SEMS,)),
            pltpu.SemaphoreType.DMA((SEMS,)),
            pltpu.SemaphoreType.DMA((4,)),
        ],
        compiler_params=pltpu.CompilerParams(
            collective_id=0, has_side_effects=True, vmem_limit_bytes=63 * 1024 * 1024
        ),
    )(feat_s, feat_t, bot_s, bot_t, proto_s, proto_t)


def per_device(feat_s, feat_t, bot_s, bot_m, bot_v, bot_t, proto_s, proto_m, proto_v, proto_t):
    g_bot, g_proto = gradients(feat_s, feat_t, bot_s, bot_t, proto_s, proto_t)
    return adamw(bot_s, bot_m, bot_v, g_bot, bot_t) + adamw(
        proto_s, proto_m, proto_v, g_proto, proto_t
    )


def solution(mesh):
    rows, columns = P(("dp", "fsdp"), None), P(None, ("fsdp", "dp"))
    return jax.shard_map(
        per_device,
        mesh=mesh,
        in_specs=(rows,) * 6 + (columns,) * 4,
        out_specs=(rows,) * 4 + (columns,) * 4,
        check_vma=False,
    )
```

```python
import math

import jax
import jax.numpy as jnp
from jax import lax
from jax.experimental import pallas as pl
from jax.experimental.pallas import tpu as pltpu
from jax.sharding import PartitionSpec as P

MESH = pl.DeviceIdType.MESH
F32, BF16 = jnp.float32, jnp.bfloat16
tau_student = 0.1
tau_teacher = 0.04
bias_first = 0.99997343860111
bias_second = 0.0952078527
LOG2E = math.log2(math.e)
PB = 256
NB = 8
NP = PB * NB
TB = 128
NT = 16 * TB
SEMS = 160


def adamw(param, first, second, grad, teacher):
    first_new = 0.9 * first + 0.1 * grad
    second_new = 0.999 * second + 0.001 * grad * grad
    direction = first_new / bias_first / (jnp.sqrt(second_new / bias_second) + 1e-08)
    param_new = param - 0.002 * (direction + 0.04 * param)
    teacher_new = 0.996 * teacher + 0.004 * param_new
    return (param_new, first_new, second_new, teacher_new)


def together(*steps):
    steps = list(steps)
    while steps:
        for step in list(steps):
            try:
                next(step)
            except StopIteration:
                steps.remove(step)
        yield


def run(*steps):
    for _ in together(*steps):
        pass


def dot(a, b, dims=((1,), (0,))):
    return lax.dot_general(a, b, (dims, ((), ())), preferred_element_type=F32)


def kernel(
    feat_s, feat_t, bot_s, bot_t, proto_s, proto_t,
    g_bot, g_proto,
    w, fx, yf, yr, unit, norm, cs, ct, ps, pt, pn, es, et, dz,
    tx, ty, tot, dh0, dhr0, dh1, dhr1, dht, grecv, gz, gzr,
    dy, b0, br0, b1, br1, b2, br2,
    send_sem, recv_sem, local_sem,
):
    dp, fs = lax.axis_index("dp"), lax.axis_index("fsdp")
    core, zl = lax.rem(dp, 2), lax.div(dp, 2)
    zh, x, y = lax.div(fs, 16), lax.rem(lax.div(fs, 4), 4), lax.rem(fs, 4)
    z = zh * 2 + zl
    other = 1 - core
    turn = 1 + 2 * core

    def device(x=x, y=y, z=z, core=core):
        return {"dp": lax.rem(z, 2) * 2 + core, "fsdp": lax.div(z, 2) * 16 + x * 4 + y}

    place = {"x": x, "y": y, "z": z}

    def ring(axis):
        at = place[axis]
        ahead, behind = lax.rem(at + turn, 4), lax.rem(at + 4 - turn, 4)
        return at, ahead, behind, lax.rem(at + 2, 4)

    copies = []

    def push(src, dst, to, log=None):
        at = len(copies)
        copy = pltpu.make_async_remote_copy(
            src_ref=src, dst_ref=dst, send_sem=send_sem.at[at], recv_sem=recv_sem.at[at],
            device_id=to, device_id_type=MESH,
        )
        copy.start()
        copies.append(copy)
        if log is not None:
            log.append(copy)
        return copy

    def gather(axis, block, log=None):
        at, ahead, behind, _ = ring(axis)
        up = push(block(at), block(at), device(**{axis: ahead}), log)
        down = push(block(at), block(at), device(**{axis: behind}), log)
        yield
        up.wait_recv()
        on = push(block(behind), block(behind), device(**{axis: ahead}), log)
        yield
        down.wait_recv()
        on.wait_recv()

    def spread(axis, block, log=None):
        at = place[axis]
        sent = []
        for d in (2, 1, 3):
            sent.append(push(block(at), block(at), device(**{axis: lax.rem(at + d, 4)}), log))
        yield
        for copy in sent:
            copy.wait_recv()

    def scatter(axis, parts, recv, put):
        at = place[axis]
        sent = []
        for i, d in enumerate((2, 1, 3)):
            to = lax.rem(at + d, 4)
            sent.append(push(parts.at[to], recv.at[i], device(**{axis: to})))
        yield
        total = parts[at].astype(F32)
        for i, copy in enumerate(sent):
            copy.wait_recv()
            total += recv[i].astype(F32)
        put(total)

    barrier = pltpu.get_barrier_semaphore()
    peers = [device(core=other)]
    for axis in ("x", "y", "z"):
        for step in (1, 2, 3):
            peers.append(device(**{axis: lax.rem(place[axis] + step, 4)}))
    for peer in peers:
        pl.semaphore_signal(barrier, inc=1, device_id=peer, device_id_type=MESH)

    local = []
    for side, feat in enumerate((feat_s, feat_t)):
        for half in range(2):
            columns = pl.ds(pl.multiple_of((half * 2 + core) * 1536, 1536), 1536)
            rows = pl.ds(pl.multiple_of(core * TB, TB), TB)
            copy = pltpu.make_async_copy(
                feat.at[:, columns], fx.at[side, half, rows, :], local_sem.at[side * 2 + half]
            )
            copy.start()
            local.append(copy)
    w[zl, zh, x, y, :, 0:256] = bot_s[...].astype(BF16)
    w[zl, zh, x, y, :, 256:512] = bot_t[...].astype(BF16)
    pl.semaphore_wait(barrier, len(peers))

    def part(k):
        return pl.ds(16 * k, 16)

    mine = {0: [], 1: []}

    def bot_gather(k, side):
        r, c = part(k), pl.ds(256 * side, 256)

        def at_z(i):
            return lax.rem(i, 2), lax.div(i, 2)

        log = mine[side]
        if k == 0:
            yield from spread("x", lambda i: w.at[zl, zh, i, y, r, c], log)
            yield from spread("y", lambda i: w.at[zl, zh, :, i, r, c], log)
            yield from gather("z", lambda i: w.at[(*at_z(i), slice(None), slice(None), r, c)], log)
        elif k == 1:
            yield from spread("y", lambda i: w.at[zl, zh, x, i, r, c], log)
            yield from spread("z", lambda i: w.at[(*at_z(i), x, slice(None), r, c)], log)
            yield from gather("x", lambda i: w.at[:, :, i, :, r, c], log)
        else:
            yield from spread("z", lambda i: w.at[(*at_z(i), x, y, r, c)], log)
            yield from spread("x", lambda i: w.at[:, :, i, y, r, c], log)
            yield from gather("y", lambda i: w.at[:, :, :, i, r, c], log)

    features = []
    for side, feat in enumerate((feat_s, feat_t)):
        for half in range(2):
            columns = pl.ds(pl.multiple_of((half * 2 + other) * 1536, 1536), 1536)
            rows = pl.ds(pl.multiple_of(core * TB, TB), TB)
            features.append((side, feat.at[:, columns], fx.at[side, half, rows, :]))
    got = {}

    def projected(side):
        yield from together(*(bot_gather(k, side) for k in range(3)))
        for copy in got[side]:
            copy.wait_recv()
        for copy in local[2 * side : 2 * side + 2]:
            copy.wait()
        total = jnp.zeros((2 * TB, 256), F32)
        for a in range(2):
            for b in range(2):
                block = w[a, b, :, :, :, pl.ds(256 * side, 256)].reshape(768, 256)
                total += dot(fx[side, a, :, pl.ds(768 * b, 768)], block)
        yf[side, 0] = total[:TB]
        yf[side, 1] = total[TB:]
        swap = push(yf.at[side, other], yr.at[side], device(core=other))
        yield
        swap.wait_recv()
        yt = (yf[side, core] + yr[side]).T
        n = jnp.sqrt(jnp.sum(yt * yt, axis=0, keepdims=True) + 1e-06)
        u = yt / n
        if side == 0:
            unit[...] = u
            norm[0:1, :] = n
        (cs, ct)[side][x, y] = u.T.astype(BF16)

    def exponentials(side, line):
        code, proto, out, scale = (
            (cs, ps, es, LOG2E / tau_student),
            (ct, pt, et, LOG2E / tau_teacher),
        )[side]

        def pair(q, _):
            if side == 0:
                c = code[pl.ds(2 * q, 2), line].reshape(2 * TB, 256)
            else:
                c = code[line, pl.ds(2 * q, 2)].reshape(2 * TB, 256)
            total = jnp.zeros((8, 2 * TB), F32)
            for b in range(NB):
                rows = pl.ds(b * PB, PB)
                e = jnp.exp2(dot(proto[b // 2, b % 2], c, ((1,), (1,))) * scale)
                if side == 0:
                    columns = pl.ds(pl.multiple_of(lax.rem(line, 2) * TB, TB), TB)
                    out[2 * q, lax.div(line, 2), rows, columns] = e[:, :TB]
                    out[2 * q + 1, lax.div(line, 2), rows, columns] = e[:, TB:]
                else:
                    out[line, q, rows, :] = e
                total += jnp.sum(e.reshape(PB // 8, 8, 2 * TB), axis=0)
            total = jnp.sum(total, axis=0, keepdims=True)
            if side == 0:
                tx[x, side, pl.ds(8 * q + line, 1), :] = total[:, :TB]
                tx[x, side, pl.ds(8 * q + 4 + line, 1), :] = total[:, TB:]
            else:
                tx[x, side, pl.ds(4 * line + 2 * q, 1), :] = total[:, :TB]
                tx[x, side, pl.ds(4 * line + 2 * q + 1, 1), :] = total[:, TB:]
            return 0

        lax.fori_loop(0, 2, pair, 0)

    def forward(side):
        yield from projected(side)
        if side == 0:
            yield from spread("x", lambda i: cs.at[i, y])
            axis, block = "y", lambda i, h: cs.at[pl.ds(2 * h, 2), i]
        else:
            yield from spread("y", lambda i: ct.at[x, i])
            axis, block = "x", lambda i, h: ct.at[i, pl.ds(2 * h, 2)]
        at, ahead, behind, far = ring(axis)
        up = [push(block(at, h), block(at, h), device(**{axis: ahead})) for h in range(2)]
        down = [push(block(at, h), block(at, h), device(**{axis: behind})) for h in range(2)]
        yield
        on = []
        for h in range(2):
            up[h].wait_recv()
            on.append(push(block(behind, h), block(behind, h), device(**{axis: ahead})))
        yield
        exponentials(side, at)
        exponentials(side, behind)
        yield
        for copy in down:
            copy.wait_recv()
        exponentials(side, ahead)
        yield
        for copy in on:
            copy.wait_recv()
        exponentials(side, far)

    def beside():
        for side, src, dst in features:
            got.setdefault(side, []).append(push(src, dst, device(core=other)))
        ps[z, core] = proto_s[...].T.astype(BF16)
        pt[z, core] = proto_t[...].T.astype(BF16)
        yield
        yield
        steps = [gather("z", lambda c, ref=ref: ref.at[c, core]) for ref in (ps, pt)]
        for step in steps:
            next(step)
        yield
        yield
        for step in steps:
            next(step)
        yield
        for copy in mine[0]:
            copy.wait_send()
        for a in range(2):
            for b in range(2):
                block = fx[0, a, :, pl.ds(768 * b, 768)].T
                w[a, b, :, :, :, 0:256] = block.reshape(4, 4, 48, 256)
        yield
        for step in steps:
            run(step)
        swaps = [push(ref.at[:, core], ref.at[:, core], device(core=other)) for ref in (ps, pt)]
        yield
        for copy in swaps:
            copy.wait_recv()
        for b in range(NB):
            pn[:, b * PB : (b + 1) * PB] = ps[b // 2, b % 2].T

    run(forward(0), forward(1), beside())

    sent = [push(tx.at[x], tx.at[x], device(x=lax.rem(x + d, 4))) for d in (1, 2, 3)]
    for copy in sent:
        copy.wait_recv()
    ty[y] = tx[0] + tx[1] + tx[2] + tx[3]
    sent = [push(ty.at[y], ty.at[y], device(y=lax.rem(y + d, 4))) for d in (1, 2, 3)]
    for copy in sent:
        copy.wait_recv()
    tot[...] = (1.0 / tau_student) / (ty[0] + ty[1] + ty[2] + ty[3])

    def back(a, h):
        i = a * 2 + h
        inv_s = jnp.concatenate([tot[0, pl.ds(2 * i, 1), :], tot[0, pl.ds(2 * i + 1, 1), :]], 1)
        inv_t = jnp.concatenate([tot[1, pl.ds(2 * i, 1), :], tot[1, pl.ds(2 * i + 1, 1), :]], 1)
        columns = pl.ds(pl.multiple_of(i * 2 * TB, 2 * TB), 2 * TB)
        dh = jnp.zeros((256, 2 * TB), F32)
        for b in range(NB):
            rows = pl.ds(b * PB, PB)
            d = (es[a, h, rows, :] * inv_s - et[a, h, rows, :] * inv_t).astype(BF16)
            dz[rows, columns] = d
            dh += dot(pn[:, rows], d)
        for d in range(2):
            dh0[0, a, 2 * h + d] = dh[:128, d * TB : (d + 1) * TB].astype(BF16)
            dh0[1, 2 * h + d, a] = dh[128:, d * TB : (d + 1) * TB].astype(BF16)

    sent = []
    for i, d in enumerate((2, 1, 3, 0)):
        to = lax.rem(x + d, 4)

        def half(h, _, to=to):
            back(to, h)
            return 0

        lax.fori_loop(0, 2, half, 0)
        if d > 0:
            sent.append(push(dh0.at[0, to], dhr0.at[0, i], device(x=to)))

    def dh_scatter(k):
        def middle(v):
            dh1[k] = v

        def last(v):
            dht[k] = v

        if k == 0:
            yield
            total = dh0[0, x].astype(F32)
            for i, copy in enumerate(sent):
                copy.wait_recv()
                total += dhr0[0, i].astype(F32)
            middle(total)
        else:
            yield from scatter("y", dh0.at[1], dhr0.at[1], middle)
        yield from scatter("yx"[k], dh1.at[k], dhr1.at[k], last)

    def proto_grad():
        def grad(block):
            rows = pl.ds(pl.multiple_of(block * PB, PB), PB)
            return dot(dz[rows, :], cs[...].reshape(NT, 256))

        def theirs(i, _):
            es[0, 0, pl.ds(pl.multiple_of(i * PB, PB), PB), :] = grad(i * 2 + other)
            return 0

        def ours(i, _):
            es[0, 1, pl.ds(pl.multiple_of(i * PB, PB), PB), :] = grad(i * 2 + core)
            return 0

        lax.fori_loop(0, 4, theirs, 0)
        swap = push(es.at[0, 0, pl.ds(0, 4 * PB), :], grecv, device(core=other))
        yield
        lax.fori_loop(0, 4, ours, 0)
        swap.wait_recv()
        gz[...] = (es[0, 1, : 4 * PB, :] + grecv[...]).astype(BF16).reshape(4, PB, 256)

        def last(v):
            g_proto[...] = v.T

        yield from scatter("z", gz, gzr, last)

    proto_steps = proto_grad()
    dh_steps = together(dh_scatter(0), dh_scatter(1))
    next(dh_steps)
    next(proto_steps)
    next(dh_steps)
    next(proto_steps)
    run(dh_steps)

    dhv = jnp.concatenate([dht[0], dht[1]], axis=0)
    u = unit[...]
    dyt = (dhv - u * jnp.sum(u * dhv, axis=0, keepdims=True)) / norm[0:1, :]
    dy[core] = dyt.astype(BF16)
    swap = push(dy.at[core], dy.at[core], device(core=other))
    swap.wait_recv()

    dyb = jnp.concatenate([dy[0], dy[1]], axis=1)
    for a in range(2):
        for b in range(2):
            c = b * 2 + a
            g = dot(w[a, b, :, :, :, 0:256].reshape(768, 256), dyb, ((1,), (1,))).astype(BF16)
            g = g.reshape(4, 4, 48, 256)
            for i in range(4):
                for j in range(4):
                    b0[0, i, j, c] = g[i, j, 0:16]
                    b0[1, j, c, i] = g[i, j, 16:32]
                    b0[2, c, i, j] = g[i, j, 32:48]

    def bot_scatter(k):
        def first(v):
            b1[k] = v

        def second(v):
            b2[k] = v

        def last(v):
            g_bot[16 * k : 16 * (k + 1), :] = v

        one, two, three = ("xyz", "yzx", "zxy")[k]
        yield from scatter(one, b0.at[k], br0.at[k], first)
        yield from scatter(two, b1.at[k], br1.at[k], second)
        yield from scatter(three, b2.at[k], br2.at[k], last)

    run(bot_scatter(0), bot_scatter(1), bot_scatter(2), proto_steps)
    for copy in copies:
        if not any(copy is one for one in mine[0]):
            copy.wait_send()


def gradients(feat_s, feat_t, bot_s, bot_t, proto_s, proto_t):
    whole = pl.BlockSpec(memory_space=pltpu.VMEM)
    vmem = pltpu.VMEM
    return pl.pallas_call(
        kernel,
        out_shape=(
            jax.ShapeDtypeStruct((48, 256), F32),
            jax.ShapeDtypeStruct((256, PB), F32),
        ),
        in_specs=[pl.BlockSpec(memory_space=pl.ANY)] * 2 + [whole] * 4,
        out_specs=(whole, whole),
        scratch_shapes=[
            vmem((2, 2, 4, 4, 48, 512), BF16),
            vmem((2, 2, 2 * TB, 1536), BF16),
            vmem((2, 2, TB, 256), F32),
            vmem((2, TB, 256), F32),
            vmem((256, TB), F32),
            vmem((8, TB), F32),
            vmem((4, 4, TB, 256), BF16),
            vmem((4, 4, TB, 256), BF16),
            vmem((4, 2, PB, 256), BF16),
            vmem((4, 2, PB, 256), BF16),
            vmem((256, NP), BF16),
            vmem((4, 2, NP, 2 * TB), F32),
            vmem((4, 2, NP, 2 * TB), F32),
            vmem((NP, NT), BF16),
            vmem((4, 2, 16, TB), F32),
            vmem((4, 2, 16, TB), F32),
            vmem((2, 16, TB), F32),
            vmem((2, 4, 4, 128, TB), BF16),
            vmem((2, 3, 4, 128, TB), BF16),
            vmem((2, 4, 128, TB), F32),
            vmem((2, 3, 128, TB), F32),
            vmem((2, 128, TB), F32),
            vmem((4 * PB, 256), F32),
            vmem((4, PB, 256), BF16),
            vmem((3, PB, 256), BF16),
            vmem((2, 256, TB), BF16),
            vmem((3, 4, 4, 4, 16, 256), BF16),
            vmem((3, 3, 4, 4, 16, 256), BF16),
            vmem((3, 4, 4, 16, 256), F32),
            vmem((3, 3, 4, 16, 256), F32),
            vmem((3, 4, 16, 256), F32),
            vmem((3, 3, 16, 256), F32),
            pltpu.SemaphoreType.DMA((SEMS,)),
            pltpu.SemaphoreType.DMA((SEMS,)),
            pltpu.SemaphoreType.DMA((4,)),
        ],
        compiler_params=pltpu.CompilerParams(
            collective_id=0, has_side_effects=True, vmem_limit_bytes=63 * 1024 * 1024
        ),
    )(feat_s, feat_t, bot_s, bot_t, proto_s, proto_t)


def per_device(feat_s, feat_t, bot_s, bot_m, bot_v, bot_t, proto_s, proto_m, proto_v, proto_t):
    g_bot, g_proto = gradients(feat_s, feat_t, bot_s, bot_t, proto_s, proto_t)
    return adamw(bot_s, bot_m, bot_v, g_bot, bot_t) + adamw(
        proto_s, proto_m, proto_v, g_proto, proto_t
    )


def solution(mesh):
    rows, columns = P(("dp", "fsdp"), None), P(None, ("fsdp", "dp"))
    return jax.shard_map(
        per_device,
        mesh=mesh,
        in_specs=(rows,) * 6 + (columns,) * 4,
        out_specs=(rows,) * 4 + (columns,) * 4,
        check_vma=False,
    )
```

```python
import math

import jax
import jax.numpy as jnp
from jax import lax
from jax.experimental import pallas as pl
from jax.experimental.pallas import tpu as pltpu
from jax.sharding import PartitionSpec as P

MESH = pl.DeviceIdType.MESH
F32, BF16 = jnp.float32, jnp.bfloat16
tau_student = 0.1
tau_teacher = 0.04
bias_first = 0.99997343860111
bias_second = 0.0952078527
LOG2E = math.log2(math.e)
PB = 256
NB = 8
NP = PB * NB
TB = 128
NT = 16 * TB
SEMS = 232


def adamw(param, first, second, grad, teacher):
    first_new = 0.9 * first + 0.1 * grad
    second_new = 0.999 * second + 0.001 * grad * grad
    direction = first_new / bias_first / (jnp.sqrt(second_new / bias_second) + 1e-08)
    param_new = param - 0.002 * (direction + 0.04 * param)
    teacher_new = 0.996 * teacher + 0.004 * param_new
    return (param_new, first_new, second_new, teacher_new)


def together(*steps):
    steps = list(steps)
    while steps:
        for step in list(steps):
            try:
                next(step)
            except StopIteration:
                steps.remove(step)
        yield


def run(*steps):
    for _ in together(*steps):
        pass


def dot(a, b, dims=((1,), (0,))):
    return lax.dot_general(a, b, (dims, ((), ())), preferred_element_type=F32)


def kernel(
    feat_s, feat_t, bot_s, bot_t, proto_s, proto_t,
    g_bot_out, g_proto_out,
    bots, protos, g_bot, g_proto,
    w, fx, yf, yr, unit, norm, cs, ct, ps, pt, pn, es, et, dz,
    tx, ty, tot, dh0, dhr0, dh1, dhr1, dht, grecv, gz, gzr,
    dy, b0, br0, b1, br1, b2, br2,
    send_sem, recv_sem, local_sem,
):
    dp, fs = lax.axis_index("dp"), lax.axis_index("fsdp")
    core, zl = lax.rem(dp, 2), lax.div(dp, 2)
    zh, x, y = lax.div(fs, 16), lax.rem(lax.div(fs, 4), 4), lax.rem(fs, 4)
    z = zh * 2 + zl
    other = 1 - core
    turn = 1 + 2 * core

    def device(x=x, y=y, z=z, core=core):
        return {"dp": lax.rem(z, 2) * 2 + core, "fsdp": lax.div(z, 2) * 16 + x * 4 + y}

    place = {"x": x, "y": y, "z": z}

    def ring(axis):
        at = place[axis]
        ahead, behind = lax.rem(at + turn, 4), lax.rem(at + 4 - turn, 4)
        return at, ahead, behind, lax.rem(at + 2, 4)

    copies = []

    def push(src, dst, to, log=None):
        at = len(copies)
        copy = pltpu.make_async_remote_copy(
            src_ref=src, dst_ref=dst, send_sem=send_sem.at[at], recv_sem=recv_sem.at[at],
            device_id=to, device_id_type=MESH,
        )
        copy.start()
        copies.append(copy)
        if log is not None:
            log.append(copy)
        return copy

    def gather(axis, block, log=None):
        at, ahead, behind, _ = ring(axis)
        up = push(block(at), block(at), device(**{axis: ahead}), log)
        down = push(block(at), block(at), device(**{axis: behind}), log)
        yield
        up.wait_recv()
        on = push(block(behind), block(behind), device(**{axis: ahead}), log)
        yield
        down.wait_recv()
        on.wait_recv()

    def spread(axis, block, log=None):
        at = place[axis]
        sent = []
        for d in (2, 1, 3):
            sent.append(push(block(at), block(at), device(**{axis: lax.rem(at + d, 4)}), log))
        yield
        for copy in sent:
            copy.wait_recv()

    def scatter(axis, parts, recv, put):
        at = place[axis]
        sent = []
        for i, d in enumerate((2, 1, 3)):
            to = lax.rem(at + d, 4)
            sent.append(push(parts.at[to], recv.at[i], device(**{axis: to})))
        yield
        total = parts[at].astype(F32)
        for i, copy in enumerate(sent):
            copy.wait_recv()
            total += recv[i].astype(F32)
        put(total)

    def load(src, dst, at):
        copy = pltpu.make_async_copy(src, dst, local_sem.at[at])
        copy.start()
        return copy

    loads = [
        load(bot_s, bots.at[0], 4),
        load(bot_t, bots.at[1], 5),
        load(proto_s, protos.at[0], 6),
        load(proto_t, protos.at[1], 7),
    ]

    barrier = pltpu.get_barrier_semaphore()
    peers = [device(core=other)]
    for axis in ("x", "y", "z"):
        for step in (1, 2, 3):
            peers.append(device(**{axis: lax.rem(place[axis] + step, 4)}))
    for peer in peers:
        pl.semaphore_signal(barrier, inc=1, device_id=peer, device_id_type=MESH)

    local = []
    for side, feat in enumerate((feat_s, feat_t)):
        for half in range(2):
            columns = pl.ds(pl.multiple_of((half * 2 + core) * 1536, 1536), 1536)
            rows = pl.ds(pl.multiple_of(core * TB, TB), TB)
            local.append(load(feat.at[:, columns], fx.at[side, half, rows, :], side * 2 + half))
    loads[0].wait()
    loads[1].wait()
    w[zl, zh, x, y, :, 0:256] = bots[0].astype(BF16)
    w[zl, zh, x, y, :, 256:512] = bots[1].astype(BF16)
    pl.semaphore_wait(barrier, len(peers))

    def part(k):
        return pl.ds(16 * k, 16)

    mine = {0: [], 1: []}

    def bot_gather(k, side):
        log, columns, every = mine[side], pl.ds(256 * side, 256), slice(None)
        one, two, three = ("xyz", "yzx", "zxy")[k]

        def block(**at):
            at = {**place, **at}
            zs = (every, every) if at["z"] is every else (lax.rem(at["z"], 2), lax.div(at["z"], 2))
            return w.at[(*zs, at["x"], at["y"], part(k), columns)]

        def send(ref, to, at):
            return push(ref, ref, device(**{to: at}), log)

        yield from spread(one, lambda i: block(**{one: i}), log)
        at = place[two]
        _, ahead, behind, _ = ring(three)
        line = block(**{one: every})
        sent = {d: send(line, two, lax.rem(at + d, 4)) for d in (2, 1, 3)}
        up, down, lines = [send(line, three, ahead)], [send(line, three, behind)], [at]
        yield
        for d in (1, 3, 2):
            sent[d].wait_recv()
            lines.append(lax.rem(at + 4 - d, 4))
            line = block(**{one: every, two: lines[-1]})
            up.append(send(line, three, ahead))
            down.append(send(line, three, behind))
        yield
        on = []
        for copy, i in zip(up, lines):
            copy.wait_recv()
            on.append(send(block(**{one: every, two: i, three: behind}), three, ahead))
        yield
        for copy in down + on:
            copy.wait_recv()

    features = []
    for side, feat in enumerate((feat_s, feat_t)):
        for half in range(2):
            columns = pl.ds(pl.multiple_of((half * 2 + other) * 1536, 1536), 1536)
            rows = pl.ds(pl.multiple_of(core * TB, TB), TB)
            features.append((side, feat.at[:, columns], fx.at[side, half, rows, :]))
    got = {}

    def projected(side):
        yield from together(*(bot_gather(k, side) for k in range(3)))
        for copy in got[side]:
            copy.wait_recv()
        for copy in local[2 * side : 2 * side + 2]:
            copy.wait()
        total = jnp.zeros((2 * TB, 256), F32)
        for a in range(2):
            for b in range(2):
                block = w[a, b, :, :, :, pl.ds(256 * side, 256)].reshape(768, 256)
                total += dot(fx[side, a, :, pl.ds(768 * b, 768)], block)
        yf[side, 0] = total[:TB]
        yf[side, 1] = total[TB:]
        swap = push(yf.at[side, other], yr.at[side], device(core=other))
        yield
        swap.wait_recv()
        yt = (yf[side, core] + yr[side]).T
        n = jnp.sqrt(jnp.sum(yt * yt, axis=0, keepdims=True) + 1e-06)
        u = yt / n
        if side == 0:
            unit[...] = u
            norm[0:1, :] = n
        (cs, ct)[side][x, y] = u.T.astype(BF16)

    def exponentials(side, line):
        code, proto, out, scale = (
            (cs, ps, es, LOG2E / tau_student),
            (ct, pt, et, LOG2E / tau_teacher),
        )[side]

        def pair(q, _):
            if side == 0:
                c = code[pl.ds(2 * q, 2), line].reshape(2 * TB, 256)
            else:
                c = code[line, pl.ds(2 * q, 2)].reshape(2 * TB, 256)
            total = jnp.zeros((8, 2 * TB), F32)
            for b in range(NB):
                rows = pl.ds(b * PB, PB)
                e = jnp.exp2(dot(proto[b // 2, b % 2], c, ((1,), (1,))) * scale)
                if side == 0:
                    columns = pl.ds(pl.multiple_of(lax.rem(line, 2) * TB, TB), TB)
                    out[2 * q, lax.div(line, 2), rows, columns] = e[:, :TB]
                    out[2 * q + 1, lax.div(line, 2), rows, columns] = e[:, TB:]
                else:
                    out[line, q, rows, :] = e
                total += jnp.sum(e.reshape(PB // 8, 8, 2 * TB), axis=0)
            total = jnp.sum(total, axis=0, keepdims=True)
            if side == 0:
                tx[x, side, pl.ds(8 * q + line, 1), :] = total[:, :TB]
                tx[x, side, pl.ds(8 * q + 4 + line, 1), :] = total[:, TB:]
            else:
                tx[x, side, pl.ds(4 * line + 2 * q, 1), :] = total[:, :TB]
                tx[x, side, pl.ds(4 * line + 2 * q + 1, 1), :] = total[:, TB:]
            return 0

        lax.fori_loop(0, 2, pair, 0)

    def forward(side):
        yield from projected(side)
        one, two = ("xy", "yx")[side]
        code = (cs, ct)[side]

        def send(i, j, to, at):
            ref = code.at[i, j] if side == 0 else code.at[j, i]
            return push(ref, ref, device(**{to: at}))

        first = place[one]
        at, ahead, behind, far = ring(two)
        sent = {d: send(first, at, one, lax.rem(first + d, 4)) for d in (2, 1, 3)}
        up, down, lines = [send(first, at, two, ahead)], [send(first, at, two, behind)], [first]
        yield
        for d in (1, 3, 2):
            sent[d].wait_recv()
            lines.append(lax.rem(first + 4 - d, 4))
            up.append(send(lines[-1], at, two, ahead))
            down.append(send(lines[-1], at, two, behind))
        yield
        on = []
        for copy, i in zip(up, lines):
            copy.wait_recv()
            on.append(send(i, behind, two, ahead))
        yield
        exponentials(side, at)
        exponentials(side, behind)
        for copy in down:
            copy.wait_recv()
        exponentials(side, ahead)
        yield
        for copy in on:
            copy.wait_recv()
        exponentials(side, far)

    def beside():
        for side, src, dst in features:
            got.setdefault(side, []).append(push(src, dst, device(core=other)))
        loads[2].wait()
        loads[3].wait()
        ps[z, core] = protos[0].T.astype(BF16)
        pt[z, core] = protos[1].T.astype(BF16)
        yield
        yield
        yield
        steps = [gather("z", lambda c, ref=ref: ref.at[c, core]) for ref in (ps, pt)]
        for step in steps:
            next(step)
        yield
        yield
        yield
        for copy in mine[0]:
            copy.wait_send()
        for a in range(2):
            for b in range(2):
                block = fx[0, a, :, pl.ds(768 * b, 768)].T
                w[a, b, :, :, :, 0:256] = block.reshape(4, 4, 48, 256)
        for step in steps:
            next(step)
        yield
        for step in steps:
            run(step)
        swaps = [push(ref.at[:, core], ref.at[:, core], device(core=other)) for ref in (ps, pt)]
        yield
        for copy in swaps:
            copy.wait_recv()
        for b in range(NB):
            pn[:, b * PB : (b + 1) * PB] = ps[b // 2, b % 2].T

    run(forward(0), forward(1), beside())

    sent = [push(tx.at[x], tx.at[x], device(x=lax.rem(x + d, 4))) for d in (2, 1, 3)]
    for copy in sent:
        copy.wait_recv()
    ty[y] = tx[0] + tx[1] + tx[2] + tx[3]
    sent = [push(ty.at[y], ty.at[y], device(y=lax.rem(y + d, 4))) for d in (2, 1, 3)]
    for copy in sent:
        copy.wait_recv()
    tot[...] = (1.0 / tau_student) / (ty[0] + ty[1] + ty[2] + ty[3])

    def back(a, h):
        i = a * 2 + h
        inv_s = jnp.concatenate([tot[0, pl.ds(2 * i, 1), :], tot[0, pl.ds(2 * i + 1, 1), :]], 1)
        inv_t = jnp.concatenate([tot[1, pl.ds(2 * i, 1), :], tot[1, pl.ds(2 * i + 1, 1), :]], 1)
        columns = pl.ds(pl.multiple_of(i * 2 * TB, 2 * TB), 2 * TB)
        dh = jnp.zeros((256, 2 * TB), F32)
        for b in range(NB):
            rows = pl.ds(b * PB, PB)
            d = (es[a, h, rows, :] * inv_s - et[a, h, rows, :] * inv_t).astype(BF16)
            dz[rows, columns] = d
            dh += dot(pn[:, rows], d)
        dh = dh.astype(BF16)
        for d in range(2):
            columns = slice(d * TB, (d + 1) * TB)
            dh0[0, a, 2 * h + d] = dh[:128, columns]
            dh0[1, 2 * h + d, a] = dh[128:, columns]

    sent, sent_y = [], []
    own, odd = lax.div(y, 2), lax.rem(y, 2)
    for h in (1 - own, own):
        for i, d in enumerate((2, 1, 3, 0)):
            to = lax.rem(x + d, 4)
            back(to, h)
            if d > 0:
                two = pl.ds(2 * h, 2)
                sent.append(push(dh0.at[0, to, two], dhr0.at[0, i, two], device(x=to)))
        if h is own:
            to = 2 * own + 1 - odd
            sent_y.append(push(dh0.at[1, to], dhr0.at[1, 0], device(y=to)))
        else:
            for e in range(2):
                to = 2 * h + lax.rem(odd + e, 2)
                sent_y.append(push(dh0.at[1, to], dhr0.at[1, 1 + e], device(y=to)))

    def dh_scatter(k):
        def middle(v):
            dh1[k] = v

        def last(v):
            dht[k] = v

        for copy in (sent, sent_y)[k]:
            copy.wait_recv()
        total = dh0[k, (x, y)[k]].astype(F32)
        for i in range(3):
            total += dhr0[k, i].astype(F32)
        middle(total)
        yield from scatter("yx"[k], dh1.at[k], dhr1.at[k], last)

    def proto_grad():
        def grad(block):
            rows = pl.ds(pl.multiple_of(block * PB, PB), PB)
            return dot(dz[rows, :], cs[...].reshape(NT, 256))

        def theirs(i, _):
            es[0, 0, pl.ds(pl.multiple_of(i * PB, PB), PB), :] = grad(i * 2 + other)
            return 0

        def ours(i, _):
            es[0, 1, pl.ds(pl.multiple_of(i * PB, PB), PB), :] = grad(i * 2 + core)
            return 0

        lax.fori_loop(0, 4, theirs, 0)
        swap = push(es.at[0, 0, pl.ds(0, 4 * PB), :], grecv, device(core=other))
        yield
        lax.fori_loop(0, 4, ours, 0)
        swap.wait_recv()
        gz[...] = (es[0, 1, : 4 * PB, :] + grecv[...]).astype(BF16).reshape(4, PB, 256)

        def last(v):
            g_proto[...] = v.T
            stores.append(load(g_proto, g_proto_out, 8))

        yield from scatter("z", gz, gzr, last)

    stores = []
    proto_steps = proto_grad()
    dh_steps = together(dh_scatter(0), dh_scatter(1))
    next(proto_steps)
    next(dh_steps)
    next(proto_steps)
    run(dh_steps)

    u = unit[...]
    dhv = jnp.concatenate([dht[0], dht[1]], axis=0)
    dyt = (dhv - u * jnp.sum(u * dhv, axis=0, keepdims=True)) / norm[0:1, :]
    dy[core] = dyt.astype(BF16)
    swap = push(dy.at[core], dy.at[core], device(core=other))
    swap.wait_recv()

    dyb = jnp.concatenate([dy[0], dy[1]], axis=1)
    for a in range(2):
        for b in range(2):
            c = b * 2 + a
            g = dot(w[a, b, :, :, :, 0:256].reshape(768, 256), dyb, ((1,), (1,))).astype(BF16)
            g = g.reshape(4, 4, 48, 256)
            for i in range(4):
                for j in range(4):
                    for h in range(2):
                        columns = slice(128 * h, 128 * (h + 1))
                        b0[h, 0, i, j, c] = g[i, j, 0:16, columns]
                        b0[h, 1, j, c, i] = g[i, j, 16:32, columns]
                        b0[h, 2, c, i, j] = g[i, j, 32:48, columns]

    def bot_scatter(k, h):
        def first(v):
            b1[h, k] = v

        def second(v):
            b2[h, k] = v

        def last(v):
            g_bot[16 * k : 16 * (k + 1), 128 * h : 128 * (h + 1)] = v

        one, two, three = ("xyz", "yzx", "zxy")[k]
        yield from scatter(one, b0.at[h, k], br0.at[h, k], first)
        yield from scatter(two, b1.at[h, k], br1.at[h, k], second)
        yield from scatter(three, b2.at[h, k], br2.at[h, k], last)

    run(*(bot_scatter(k, h) for h in range(2) for k in range(3)), proto_steps)
    stores.append(load(g_bot, g_bot_out, 9))
    for copy in copies:
        if not any(copy is one for one in mine[0]):
            copy.wait_send()
    for copy in stores:
        copy.wait()


def gradients(feat_s, feat_t, bot_s, bot_t, proto_s, proto_t):
    vmem = pltpu.VMEM
    return pl.pallas_call(
        kernel,
        out_shape=(
            jax.ShapeDtypeStruct((48, 256), F32),
            jax.ShapeDtypeStruct((256, PB), F32),
        ),
        in_specs=[pl.BlockSpec(memory_space=pl.ANY)] * 6,
        out_specs=(pl.BlockSpec(memory_space=pl.ANY),) * 2,
        scratch_shapes=[
            vmem((2, 48, 256), F32),
            vmem((2, 256, PB), F32),
            vmem((48, 256), F32),
            vmem((256, PB), F32),
            vmem((2, 2, 4, 4, 48, 512), BF16),
            vmem((2, 2, 2 * TB, 1536), BF16),
            vmem((2, 2, TB, 256), F32),
            vmem((2, TB, 256), F32),
            vmem((256, TB), F32),
            vmem((8, TB), F32),
            vmem((4, 4, TB, 256), BF16),
            vmem((4, 4, TB, 256), BF16),
            vmem((4, 2, PB, 256), BF16),
            vmem((4, 2, PB, 256), BF16),
            vmem((256, NP), BF16),
            vmem((4, 2, NP, 2 * TB), F32),
            vmem((4, 2, NP, 2 * TB), F32),
            vmem((NP, NT), BF16),
            vmem((4, 2, 16, TB), F32),
            vmem((4, 2, 16, TB), F32),
            vmem((2, 16, TB), F32),
            vmem((2, 4, 4, 128, TB), BF16),
            vmem((2, 3, 4, 128, TB), BF16),
            vmem((2, 4, 128, TB), F32),
            vmem((2, 3, 128, TB), F32),
            vmem((2, 128, TB), F32),
            vmem((4 * PB, 256), F32),
            vmem((4, PB, 256), BF16),
            vmem((3, PB, 256), BF16),
            vmem((2, 256, TB), BF16),
            vmem((2, 3, 4, 4, 4, 16, 128), BF16),
            vmem((2, 3, 3, 4, 4, 16, 128), BF16),
            vmem((2, 3, 4, 4, 16, 128), F32),
            vmem((2, 3, 3, 4, 16, 128), F32),
            vmem((2, 3, 4, 16, 128), F32),
            vmem((2, 3, 3, 16, 128), F32),
            pltpu.SemaphoreType.DMA((SEMS,)),
            pltpu.SemaphoreType.DMA((SEMS,)),
            pltpu.SemaphoreType.DMA((10,)),
        ],
        compiler_params=pltpu.CompilerParams(
            collective_id=0, has_side_effects=True, vmem_limit_bytes=63 * 1024 * 1024
        ),
    )(feat_s, feat_t, bot_s, bot_t, proto_s, proto_t)


def per_device(feat_s, feat_t, bot_s, bot_m, bot_v, bot_t, proto_s, proto_m, proto_v, proto_t):
    g_bot, g_proto = gradients(feat_s, feat_t, bot_s, bot_t, proto_s, proto_t)
    return adamw(bot_s, bot_m, bot_v, g_bot, bot_t) + adamw(
        proto_s, proto_m, proto_v, g_proto, proto_t
    )


def solution(mesh):
    rows, columns = P(("dp", "fsdp"), None), P(None, ("fsdp", "dp"))
    return jax.shard_map(
        per_device,
        mesh=mesh,
        in_specs=(rows,) * 6 + (columns,) * 4,
        out_specs=(rows,) * 4 + (columns,) * 4,
        check_vma=False,
    )
```

```python
import math

import jax
import jax.numpy as jnp
from jax import lax
from jax.experimental import pallas as pl
from jax.experimental.pallas import tpu as pltpu
from jax.sharding import PartitionSpec as P

MESH = pl.DeviceIdType.MESH
F32, BF16 = jnp.float32, jnp.bfloat16
tau_student = 0.1
tau_teacher = 0.04
bias_first = 0.99997343860111
bias_second = 0.0952078527
LOG2E = math.log2(math.e)
PB = 256
NB = 8
NP = PB * NB
TB = 128
NT = 16 * TB
SEMS = 256


def adamw(param, first, second, grad, teacher):
    first_new = 0.9 * first + 0.1 * grad
    second_new = 0.999 * second + 0.001 * grad * grad
    direction = first_new / bias_first / (jnp.sqrt(second_new / bias_second) + 1e-08)
    param_new = param - 0.002 * (direction + 0.04 * param)
    teacher_new = 0.996 * teacher + 0.004 * param_new
    return (param_new, first_new, second_new, teacher_new)


def together(*steps):
    steps = list(steps)
    while steps:
        for step in list(steps):
            try:
                next(step)
            except StopIteration:
                steps.remove(step)
        yield


def run(*steps):
    for _ in together(*steps):
        pass


def dot(a, b, dims=((1,), (0,))):
    return lax.dot_general(a, b, (dims, ((), ())), preferred_element_type=F32)


def kernel(
    feat_s, feat_t, bot_s, bot_t, proto_s, proto_t,
    g_bot_out, g_proto_out,
    bots, protos, g_bot, g_proto,
    w, fx, yf, yr, unit, norm, cs, ct, ps, pt, pn, es, et, dz,
    tx, ty, tot, dh0, dhr0, dh1, dhr1, dht, grecv, gz, gzr,
    dy, b0, br0, b1, br1, b2, br2,
    send_sem, recv_sem, local_sem,
):
    dp, fs = lax.axis_index("dp"), lax.axis_index("fsdp")
    core, zl = lax.rem(dp, 2), lax.div(dp, 2)
    zh, x, y = lax.div(fs, 16), lax.rem(lax.div(fs, 4), 4), lax.rem(fs, 4)
    z = zh * 2 + zl
    other = 1 - core
    turn = 1 + 2 * core

    def device(x=x, y=y, z=z, core=core):
        return {"dp": lax.rem(z, 2) * 2 + core, "fsdp": lax.div(z, 2) * 16 + x * 4 + y}

    place = {"x": x, "y": y, "z": z}

    def ring(axis):
        at = place[axis]
        ahead, behind = lax.rem(at + turn, 4), lax.rem(at + 4 - turn, 4)
        return at, ahead, behind, lax.rem(at + 2, 4)

    copies = []

    def push(src, dst, to, log=None):
        at = len(copies)
        copy = pltpu.make_async_remote_copy(
            src_ref=src, dst_ref=dst, send_sem=send_sem.at[at], recv_sem=recv_sem.at[at],
            device_id=to, device_id_type=MESH,
        )
        copy.start()
        copies.append(copy)
        if log is not None:
            log.append(copy)
        return copy

    def gather(axis, block, log=None):
        at, ahead, behind, _ = ring(axis)
        up = push(block(at), block(at), device(**{axis: ahead}), log)
        down = push(block(at), block(at), device(**{axis: behind}), log)
        yield
        up.wait_recv()
        on = push(block(behind), block(behind), device(**{axis: ahead}), log)
        yield
        down.wait_recv()
        on.wait_recv()

    def spread(axis, block, log=None):
        at = place[axis]
        sent = []
        for d in (2, 1, 3):
            sent.append(push(block(at), block(at), device(**{axis: lax.rem(at + d, 4)}), log))
        yield
        for copy in sent:
            copy.wait_recv()

    def scatter(axis, parts, recv, put):
        at = place[axis]
        sent = []
        for i, d in enumerate((2, 1, 3)):
            to = lax.rem(at + d, 4)
            sent.append(push(parts.at[to], recv.at[i], device(**{axis: to})))
        yield
        total = parts[at].astype(F32)
        for i, copy in enumerate(sent):
            copy.wait_recv()
            total += recv[i].astype(F32)
        put(total)

    def load(src, dst, at):
        copy = pltpu.make_async_copy(src, dst, local_sem.at[at])
        copy.start()
        return copy

    barrier = pltpu.get_barrier_semaphore()
    peers = [device(core=other)]
    for axis in ("x", "y", "z"):
        for step in (1, 2, 3):
            peers.append(device(**{axis: lax.rem(place[axis] + step, 4)}))
    for peer in peers:
        pl.semaphore_signal(barrier, inc=1, device_id=peer, device_id_type=MESH)

    loads = [
        load(bot_s, bots.at[0], 4),
        load(bot_t, bots.at[1], 5),
        load(proto_s, protos.at[0], 6),
        load(proto_t, protos.at[1], 7),
    ]

    local = []
    for side, feat in enumerate((feat_s, feat_t)):
        for half in range(2):
            columns = pl.ds(pl.multiple_of((half * 2 + core) * 1536, 1536), 1536)
            rows = pl.ds(pl.multiple_of(core * TB, TB), TB)
            local.append(load(feat.at[:, columns], fx.at[side, half, rows, :], side * 2 + half))
    loads[0].wait()
    loads[1].wait()
    w[zl, zh, x, y, :, 0:256] = bots[0].astype(BF16)
    w[zl, zh, x, y, :, 256:512] = bots[1].astype(BF16)
    pl.semaphore_wait(barrier, len(peers))

    def part(k):
        return pl.ds(16 * k, 16)

    mine = {0: [], 1: []}

    def bot_gather(k, side):
        log, columns, every = mine[side], pl.ds(256 * side, 256), slice(None)
        one, two, three = ("xyz", "yzx", "zxy")[k]

        def block(**at):
            at = {**place, **at}
            zs = (every, every) if at["z"] is every else (lax.rem(at["z"], 2), lax.div(at["z"], 2))
            return w.at[(*zs, at["x"], at["y"], part(k), columns)]

        def send(ref, to, at):
            return push(ref, ref, device(**{to: at}), log)

        yield from spread(one, lambda i: block(**{one: i}), log)
        at = place[two]
        _, ahead, behind, _ = ring(three)
        line = block(**{one: every})
        sent = {d: send(line, two, lax.rem(at + d, 4)) for d in (2, 1, 3)}
        up, down, lines = [send(line, three, ahead)], [send(line, three, behind)], [at]
        yield
        for d in (1, 3, 2):
            sent[d].wait_recv()
            lines.append(lax.rem(at + 4 - d, 4))
            line = block(**{one: every, two: lines[-1]})
            up.append(send(line, three, ahead))
            down.append(send(line, three, behind))
        yield
        on = []
        for copy, i in zip(up, lines):
            copy.wait_recv()
            on.append(send(block(**{one: every, two: i, three: behind}), three, ahead))
        yield
        for copy in down + on:
            copy.wait_recv()

    features = []
    for side, feat in enumerate((feat_s, feat_t)):
        for half in range(2):
            columns = pl.ds(pl.multiple_of((half * 2 + other) * 1536, 1536), 1536)
            rows = pl.ds(pl.multiple_of(core * TB, TB), TB)
            features.append((side, feat.at[:, columns], fx.at[side, half, rows, :]))
    got = {}

    def projected(side):
        yield from together(*(bot_gather(k, side) for k in range(3)))
        for copy in got[side]:
            copy.wait_recv()
        for copy in local[2 * side : 2 * side + 2]:
            copy.wait()
        total = jnp.zeros((2 * TB, 256), F32)
        for a in range(2):
            for b in range(2):
                block = w[a, b, :, :, :, pl.ds(256 * side, 256)].reshape(768, 256)
                total += dot(fx[side, a, :, pl.ds(768 * b, 768)], block)
        yf[side, 0] = total[:TB]
        yf[side, 1] = total[TB:]
        swap = push(yf.at[side, other], yr.at[side], device(core=other))
        yield
        swap.wait_recv()
        v = yf[side, core] + yr[side]
        n = jnp.sqrt(jnp.sum(v * v, axis=1, keepdims=True) + 1e-06)
        (cs, ct)[side][x, y] = (v / n).astype(BF16)

    def exponentials(side, line):
        code, proto, out, scale = (
            (cs, ps, es, LOG2E / tau_student),
            (ct, pt, et, LOG2E / tau_teacher),
        )[side]

        def pair(q, _):
            if side == 0:
                c = code[pl.ds(2 * q, 2), line].reshape(2 * TB, 256)
            else:
                c = code[line, pl.ds(2 * q, 2)].reshape(2 * TB, 256)
            total = jnp.zeros((8, 2 * TB), F32)
            for b in range(NB):
                rows = pl.ds(b * PB, PB)
                e = jnp.exp2(dot(proto[b // 2, b % 2], c, ((1,), (1,))) * scale)
                if side == 0:
                    columns = pl.ds(pl.multiple_of(lax.rem(line, 2) * TB, TB), TB)
                    out[2 * q, lax.div(line, 2), rows, columns] = e[:, :TB]
                    out[2 * q + 1, lax.div(line, 2), rows, columns] = e[:, TB:]
                else:
                    out[line, q, rows, :] = e
                total += jnp.sum(e.reshape(PB // 8, 8, 2 * TB), axis=0)
            total = jnp.sum(total, axis=0, keepdims=True)
            if side == 0:
                tx[x, side, pl.ds(8 * q + line, 1), :] = total[:, :TB]
                tx[x, side, pl.ds(8 * q + 4 + line, 1), :] = total[:, TB:]
            else:
                tx[x, side, pl.ds(4 * line + 2 * q, 1), :] = total[:, :TB]
                tx[x, side, pl.ds(4 * line + 2 * q + 1, 1), :] = total[:, TB:]
            return 0

        lax.fori_loop(0, 2, pair, 0)

    def forward(side):
        yield from projected(side)
        one, two = ("xy", "yx")[side]
        code = (cs, ct)[side]

        def send(i, j, to, at):
            ref = code.at[i, j] if side == 0 else code.at[j, i]
            return push(ref, ref, device(**{to: at}))

        first = place[one]
        at, ahead, behind, far = ring(two)
        sent = {d: send(first, at, one, lax.rem(first + d, 4)) for d in (2, 1, 3)}
        up, down, lines = [send(first, at, two, ahead)], [send(first, at, two, behind)], [first]
        yield
        for d in (1, 3, 2):
            sent[d].wait_recv()
            lines.append(lax.rem(first + 4 - d, 4))
            up.append(send(lines[-1], at, two, ahead))
            down.append(send(lines[-1], at, two, behind))
        yield
        on = []
        for copy, i in zip(up, lines):
            copy.wait_recv()
            on.append(send(i, behind, two, ahead))
        yield
        exponentials(side, at)
        exponentials(side, behind)
        for copy in down:
            copy.wait_recv()
        exponentials(side, ahead)
        yield
        for copy in on:
            copy.wait_recv()
        exponentials(side, far)

    def beside():
        for side, src, dst in features:
            got.setdefault(side, []).append(push(src, dst, device(core=other)))
        loads[2].wait()
        loads[3].wait()
        ps[z, core] = protos[0].T.astype(BF16)
        pt[z, core] = protos[1].T.astype(BF16)
        yield
        yield
        yield
        steps = [gather("z", lambda c, ref=ref: ref.at[c, core]) for ref in (ps, pt)]
        for step in steps:
            next(step)
        yield
        yield
        yield
        for copy in mine[0]:
            copy.wait_send()
        for a in range(2):
            for b in range(2):
                block = fx[0, a, :, pl.ds(768 * b, 768)].T
                w[a, b, :, :, :, 0:256] = block.reshape(4, 4, 48, 256)
        for step in steps:
            next(step)
        yield
        yt = (yf[0, core] + yr[0]).T
        n = jnp.sqrt(jnp.sum(yt * yt, axis=0, keepdims=True) + 1e-06)
        unit[...] = yt / n
        norm[0:1, :] = n
        for step in steps:
            run(step)
        swaps = [push(ref.at[:, core], ref.at[:, core], device(core=other)) for ref in (ps, pt)]
        yield
        for copy in swaps:
            copy.wait_recv()
        for b in range(NB):
            pn[:, b * PB : (b + 1) * PB] = ps[b // 2, b % 2].T

    run(forward(0), forward(1), beside())

    sent = [push(tx.at[x], tx.at[x], device(x=lax.rem(x + d, 4))) for d in (2, 1, 3)]
    for copy in sent:
        copy.wait_recv()
    ty[y] = tx[0] + tx[1] + tx[2] + tx[3]
    sent = [push(ty.at[y], ty.at[y], device(y=lax.rem(y + d, 4))) for d in (2, 1, 3)]
    for copy in sent:
        copy.wait_recv()
    tot[...] = (1.0 / tau_student) / (ty[0] + ty[1] + ty[2] + ty[3])

    def back(a, h):
        i = a * 2 + h
        inv_s = jnp.concatenate([tot[0, pl.ds(2 * i, 1), :], tot[0, pl.ds(2 * i + 1, 1), :]], 1)
        inv_t = jnp.concatenate([tot[1, pl.ds(2 * i, 1), :], tot[1, pl.ds(2 * i + 1, 1), :]], 1)
        columns = pl.ds(pl.multiple_of(i * 2 * TB, 2 * TB), 2 * TB)
        dh = jnp.zeros((256, 2 * TB), F32)
        for b in range(NB):
            rows = pl.ds(b * PB, PB)
            d = (es[a, h, rows, :] * inv_s - et[a, h, rows, :] * inv_t).astype(BF16)
            dz[rows, columns] = d
            dh += dot(pn[:, rows], d)
        dh = dh.astype(BF16)
        for d in range(2):
            columns = slice(d * TB, (d + 1) * TB)
            dh0[0, a, 2 * h + d] = dh[:128, columns]
            dh0[1, 2 * h + d, a] = dh[128:, columns]

    own, odd = lax.div(y, 2), lax.rem(y, 2)
    mate = 2 * own + 1 - odd
    across = [2 * (1 - own) + lax.rem(odd + e, 2) for e in range(2)]
    order = [(d, lax.rem(x + d, 4)) for d in (2, 1, 3, 0)]
    sent, sent_y = [[], []], []
    for n, h in enumerate((1 - own, own)):
        two = pl.ds(2 * h, 2)
        for i, (d, to) in enumerate(order):
            back(to, h)
            if d > 0:
                sent[n].append(push(dh0.at[0, to, two], dhr0.at[0, i, two], device(x=to)))
            for slot, to_y in ((1, across[0]), (2, across[1])) if n == 0 else ((0, mate),):
                sent_y.append(push(dh0.at[1, to_y, to], dhr0.at[1, slot, to], device(y=to_y)))

    passed = [[], []]

    def dh_rows(n):
        for copy in sent[n]:
            copy.wait_recv()
        for slot, to in ((1, across[0]), (2, across[1])) if n == 0 else ((0, mate), (None, y)):
            total = dh0[0, x, to].astype(F32)
            for i in range(3):
                total += dhr0[0, i, to].astype(F32)
            dh1[0, to] = total
            if slot is not None:
                passed[0].append(push(dh1.at[0, to], dhr1.at[0, slot], device(y=to)))

    def dh_columns(i):
        d, to = order[i]
        for at in (2 * i, 2 * i + 1, 8 + i):
            sent_y[at].wait_recv()
        total = dh0[1, y, to].astype(F32)
        for slot in range(3):
            total += dhr0[1, slot, to].astype(F32)
        dh1[1, to] = total
        if d > 0:
            passed[1].append(push(dh1.at[1, to], dhr1.at[1, i], device(x=to)))

    def proto_grad():
        def grad(block):
            rows = pl.ds(pl.multiple_of(block * PB, PB), PB)
            return dot(dz[rows, :], cs[...].reshape(NT, 256))

        def theirs(i, _):
            es[0, 0, pl.ds(pl.multiple_of(i * PB, PB), PB), :] = grad(i * 2 + other)
            return 0

        def ours(i, _):
            es[0, 1, pl.ds(pl.multiple_of(i * PB, PB), PB), :] = grad(i * 2 + core)
            return 0

        lax.fori_loop(0, 4, theirs, 0)
        swap = push(es.at[0, 0, pl.ds(0, 4 * PB), :], grecv, device(core=other))
        yield
        lax.fori_loop(0, 4, ours, 0)
        swap.wait_recv()
        gz[...] = (es[0, 1, : 4 * PB, :] + grecv[...]).astype(BF16).reshape(4, PB, 256)

        def last(v):
            g_proto[...] = v.T
            stores.append(load(g_proto, g_proto_out, 8))

        yield from scatter("z", gz, gzr, last)

    stores = []
    proto_steps = proto_grad()
    next(proto_steps)
    dh_rows(0)
    dh_columns(0)
    dh_columns(1)
    dh_rows(1)
    dh_columns(2)
    dh_columns(3)
    next(proto_steps)
    for k in range(2):
        for copy in passed[k]:
            copy.wait_recv()
        dht[k] = dh1[k, (y, x)[k]] + dhr1[k, 0] + dhr1[k, 1] + dhr1[k, 2]

    u = unit[...]
    dhv = jnp.concatenate([dht[0], dht[1]], axis=0)
    dyt = (dhv - u * jnp.sum(u * dhv, axis=0, keepdims=True)) / norm[0:1, :]
    dy[core] = dyt.astype(BF16)
    swap = push(dy.at[core], dy.at[core], device(core=other))
    swap.wait_recv()

    dyb = jnp.concatenate([dy[0], dy[1]], axis=1)
    for a in range(2):
        for b in range(2):
            c = b * 2 + a
            g = dot(w[a, b, :, :, :, 0:256].reshape(768, 256), dyb, ((1,), (1,))).astype(BF16)
            g = g.reshape(4, 4, 48, 256)
            for i in range(4):
                for j in range(4):
                    for h in range(2):
                        columns = slice(128 * h, 128 * (h + 1))
                        b0[h, 0, i, j, c] = g[i, j, 0:16, columns]
                        b0[h, 1, j, c, i] = g[i, j, 16:32, columns]
                        b0[h, 2, c, i, j] = g[i, j, 32:48, columns]

    def bot_scatter(k, h):
        def first(v):
            b1[h, k] = v

        def second(v):
            b2[h, k] = v

        def last(v):
            g_bot[16 * k : 16 * (k + 1), 128 * h : 128 * (h + 1)] = v

        one, two, three = ("xyz", "yzx", "zxy")[k]
        yield from scatter(one, b0.at[h, k], br0.at[h, k], first)
        yield from scatter(two, b1.at[h, k], br1.at[h, k], second)
        yield from scatter(three, b2.at[h, k], br2.at[h, k], last)

    run(*(bot_scatter(k, h) for h in range(2) for k in range(3)), proto_steps)
    stores.append(load(g_bot, g_bot_out, 9))
    for copy in copies:
        if not any(copy is one for one in mine[0]):
            copy.wait_send()
    for copy in stores:
        copy.wait()


def gradients(feat_s, feat_t, bot_s, bot_t, proto_s, proto_t):
    vmem = pltpu.VMEM
    return pl.pallas_call(
        kernel,
        out_shape=(
            jax.ShapeDtypeStruct((48, 256), F32),
            jax.ShapeDtypeStruct((256, PB), F32),
        ),
        in_specs=[pl.BlockSpec(memory_space=pl.ANY)] * 6,
        out_specs=(pl.BlockSpec(memory_space=pl.ANY),) * 2,
        scratch_shapes=[
            vmem((2, 48, 256), F32),
            vmem((2, 256, PB), F32),
            vmem((48, 256), F32),
            vmem((256, PB), F32),
            vmem((2, 2, 4, 4, 48, 512), BF16),
            vmem((2, 2, 2 * TB, 1536), BF16),
            vmem((2, 2, TB, 256), F32),
            vmem((2, TB, 256), F32),
            vmem((256, TB), F32),
            vmem((8, TB), F32),
            vmem((4, 4, TB, 256), BF16),
            vmem((4, 4, TB, 256), BF16),
            vmem((4, 2, PB, 256), BF16),
            vmem((4, 2, PB, 256), BF16),
            vmem((256, NP), BF16),
            vmem((4, 2, NP, 2 * TB), F32),
            vmem((4, 2, NP, 2 * TB), F32),
            vmem((NP, NT), BF16),
            vmem((4, 2, 16, TB), F32),
            vmem((4, 2, 16, TB), F32),
            vmem((2, 16, TB), F32),
            vmem((2, 4, 4, 128, TB), BF16),
            vmem((2, 3, 4, 128, TB), BF16),
            vmem((2, 4, 128, TB), F32),
            vmem((2, 3, 128, TB), F32),
            vmem((2, 128, TB), F32),
            vmem((4 * PB, 256), F32),
            vmem((4, PB, 256), BF16),
            vmem((3, PB, 256), BF16),
            vmem((2, 256, TB), BF16),
            vmem((2, 3, 4, 4, 4, 16, 128), BF16),
            vmem((2, 3, 3, 4, 4, 16, 128), BF16),
            vmem((2, 3, 4, 4, 16, 128), F32),
            vmem((2, 3, 3, 4, 16, 128), F32),
            vmem((2, 3, 4, 16, 128), F32),
            vmem((2, 3, 3, 16, 128), F32),
            pltpu.SemaphoreType.DMA((SEMS,)),
            pltpu.SemaphoreType.DMA((SEMS,)),
            pltpu.SemaphoreType.DMA((10,)),
        ],
        compiler_params=pltpu.CompilerParams(
            collective_id=0, has_side_effects=True, vmem_limit_bytes=63 * 1024 * 1024
        ),
    )(feat_s, feat_t, bot_s, bot_t, proto_s, proto_t)


def per_device(feat_s, feat_t, bot_s, bot_m, bot_v, bot_t, proto_s, proto_m, proto_v, proto_t):
    g_bot, g_proto = gradients(feat_s, feat_t, bot_s, bot_t, proto_s, proto_t)
    return adamw(bot_s, bot_m, bot_v, g_bot, bot_t) + adamw(
        proto_s, proto_m, proto_v, g_proto, proto_t
    )


def solution(mesh):
    rows, columns = P(("dp", "fsdp"), None), P(None, ("fsdp", "dp"))
    return jax.shard_map(
        per_device,
        mesh=mesh,
        in_specs=(rows,) * 6 + (columns,) * 4,
        out_specs=(rows,) * 4 + (columns,) * 4,
        check_vma=False,
    )
```

```python
import math

import jax
import jax.numpy as jnp
from jax import lax
from jax.experimental import pallas as pl
from jax.experimental.pallas import tpu as pltpu
from jax.sharding import PartitionSpec as P

MESH = pl.DeviceIdType.MESH
F32, BF16 = jnp.float32, jnp.bfloat16
tau_student = 0.1
tau_teacher = 0.04
bias_first = 0.99997343860111
bias_second = 0.0952078527
LOG2E = math.log2(math.e)
PB = 256
NB = 8
NP = PB * NB
TB = 128
NT = 16 * TB
SEMS = 256


def adamw(param, first, second, grad, teacher):
    first_new = 0.9 * first + 0.1 * grad
    second_new = 0.999 * second + 0.001 * grad * grad
    direction = first_new / bias_first / (jnp.sqrt(second_new / bias_second) + 1e-08)
    param_new = param - 0.002 * (direction + 0.04 * param)
    teacher_new = 0.996 * teacher + 0.004 * param_new
    return (param_new, first_new, second_new, teacher_new)


def together(*steps):
    steps = list(steps)
    while steps:
        for step in list(steps):
            try:
                next(step)
            except StopIteration:
                steps.remove(step)
        yield


def run(*steps):
    for _ in together(*steps):
        pass


def dot(a, b, dims=((1,), (0,))):
    return lax.dot_general(a, b, (dims, ((), ())), preferred_element_type=F32)


def kernel(
    feat_s, feat_t, bot_s, bot_t, proto_s, proto_t,
    g_bot_out, g_proto_out,
    bots, protos, g_bot, g_proto,
    w, fx, yf, yr, unit, norm, cs, ct, ps, pt, pn, es, et, dz,
    tx, ty, tot, dh0, dhr0, dh1, dhr1, dht, grecv, gz, gzr,
    dy, b0, br0, b1, br1, b2, br2,
    send_sem, recv_sem, local_sem,
):
    dp, fs = lax.axis_index("dp"), lax.axis_index("fsdp")
    core, zl = lax.rem(dp, 2), lax.div(dp, 2)
    zh, x, y = lax.div(fs, 16), lax.rem(lax.div(fs, 4), 4), lax.rem(fs, 4)
    z = zh * 2 + zl
    other = 1 - core
    turn = 1 + 2 * core

    def device(x=x, y=y, z=z, core=core):
        return {"dp": lax.rem(z, 2) * 2 + core, "fsdp": lax.div(z, 2) * 16 + x * 4 + y}

    place = {"x": x, "y": y, "z": z}

    def ring(axis):
        at = place[axis]
        ahead, behind = lax.rem(at + turn, 4), lax.rem(at + 4 - turn, 4)
        return at, ahead, behind, lax.rem(at + 2, 4)

    copies = []

    def push(src, dst, to, log=None):
        at = len(copies)
        copy = pltpu.make_async_remote_copy(
            src_ref=src, dst_ref=dst, send_sem=send_sem.at[at], recv_sem=recv_sem.at[at],
            device_id=to, device_id_type=MESH,
        )
        copy.start()
        copies.append(copy)
        if log is not None:
            log.append(copy)
        return copy

    def gather(axis, block, log=None):
        at, ahead, behind, _ = ring(axis)
        up = push(block(at), block(at), device(**{axis: ahead}), log)
        down = push(block(at), block(at), device(**{axis: behind}), log)
        yield
        up.wait_recv()
        on = push(block(behind), block(behind), device(**{axis: ahead}), log)
        yield
        down.wait_recv()
        on.wait_recv()

    def spread(axis, block, log=None):
        at = place[axis]
        sent = []
        for d in (2, 1, 3):
            sent.append(push(block(at), block(at), device(**{axis: lax.rem(at + d, 4)}), log))
        yield
        for copy in sent:
            copy.wait_recv()

    def scatter(axis, parts, recv, put):
        at = place[axis]
        sent = []
        for i, d in enumerate((2, 1, 3)):
            to = lax.rem(at + d, 4)
            sent.append(push(parts.at[to], recv.at[i], device(**{axis: to})))
        yield
        total = parts[at].astype(F32)
        for i, copy in enumerate(sent):
            copy.wait_recv()
            total += recv[i].astype(F32)
        put(total)

    def load(src, dst, at):
        copy = pltpu.make_async_copy(src, dst, local_sem.at[at])
        copy.start()
        return copy

    barrier = pltpu.get_barrier_semaphore()
    peers = [device(core=other)]
    for axis in ("x", "y", "z"):
        for step in (1, 2, 3):
            peers.append(device(**{axis: lax.rem(place[axis] + step, 4)}))
    for peer in peers:
        pl.semaphore_signal(barrier, inc=1, device_id=peer, device_id_type=MESH)

    loads = [
        load(bot_s, bots.at[0], 4),
        load(bot_t, bots.at[1], 5),
        load(proto_s, protos.at[0], 6),
        load(proto_t, protos.at[1], 7),
    ]

    local = []
    for side, feat in enumerate((feat_s, feat_t)):
        for half in range(2):
            columns = pl.ds(pl.multiple_of((half * 2 + core) * 1536, 1536), 1536)
            rows = pl.ds(pl.multiple_of(core * TB, TB), TB)
            local.append(load(feat.at[:, columns], fx.at[side, half, rows, :], side * 2 + half))
    loads[0].wait()
    loads[1].wait()
    w[zl, zh, x, y, :, 0:256] = bots[0].astype(BF16)
    w[zl, zh, x, y, :, 256:512] = bots[1].astype(BF16)
    pl.semaphore_wait(barrier, len(peers))

    def part(k):
        return pl.ds(16 * k, 16)

    mine = {0: [], 1: []}

    def bot_gather(k, side):
        log, columns, every = mine[side], pl.ds(256 * side, 256), slice(None)
        one, two, three = ("xyz", "yzx", "zxy")[k]

        def block(**at):
            at = {**place, **at}
            zs = (every, every) if at["z"] is every else (lax.rem(at["z"], 2), lax.div(at["z"], 2))
            return w.at[(*zs, at["x"], at["y"], part(k), columns)]

        def send(ref, to, at):
            return push(ref, ref, device(**{to: at}), log)

        yield from spread(one, lambda i: block(**{one: i}), log)
        at = place[two]
        _, ahead, behind, _ = ring(three)
        line = block(**{one: every})
        sent = {d: send(line, two, lax.rem(at + d, 4)) for d in (2, 1, 3)}
        up, down, lines = [send(line, three, ahead)], [send(line, three, behind)], [at]
        yield
        for d in (1, 3, 2):
            sent[d].wait_recv()
            lines.append(lax.rem(at + 4 - d, 4))
            line = block(**{one: every, two: lines[-1]})
            up.append(send(line, three, ahead))
            down.append(send(line, three, behind))
        yield
        on = []
        for copy, i in zip(up, lines):
            copy.wait_recv()
            on.append(send(block(**{one: every, two: i, three: behind}), three, ahead))
        yield
        for copy in down + on:
            copy.wait_recv()

    features = []
    for side, feat in enumerate((feat_s, feat_t)):
        for half in range(2):
            columns = pl.ds(pl.multiple_of((half * 2 + other) * 1536, 1536), 1536)
            rows = pl.ds(pl.multiple_of(core * TB, TB), TB)
            features.append((side, feat.at[:, columns], fx.at[side, half, rows, :]))
    got = {}

    def projected(side):
        yield from together(*(bot_gather(k, side) for k in range(3)))
        for copy in got[side]:
            copy.wait_recv()
        for copy in local[2 * side : 2 * side + 2]:
            copy.wait()
        total = jnp.zeros((2 * TB, 256), F32)
        for a in range(2):
            for b in range(2):
                block = w[a, b, :, :, :, pl.ds(256 * side, 256)].reshape(768, 256)
                total += dot(fx[side, a, :, pl.ds(768 * b, 768)], block)
        yf[side, 0] = total[:TB]
        yf[side, 1] = total[TB:]
        swap = push(yf.at[side, other], yr.at[side], device(core=other))
        yield
        swap.wait_recv()
        v = yf[side, core] + yr[side]
        n = jnp.sqrt(jnp.sum(v * v, axis=1, keepdims=True) + 1e-06)
        (cs, ct)[side][x, y] = (v / n).astype(BF16)

    def exponentials(side, line):
        code, proto, out, scale = (
            (cs, ps, es, LOG2E / tau_student),
            (ct, pt, et, LOG2E / tau_teacher),
        )[side]

        def pair(q, _):
            if side == 0:
                c = code[pl.ds(2 * q, 2), line].reshape(2 * TB, 256)
            else:
                c = code[line, pl.ds(2 * q, 2)].reshape(2 * TB, 256)
            total = jnp.zeros((8, 2 * TB), F32)
            for b in range(NB):
                rows = pl.ds(b * PB, PB)
                e = jnp.exp2(dot(proto[b // 2, b % 2], c, ((1,), (1,))) * scale)
                if side == 0:
                    columns = pl.ds(pl.multiple_of(lax.rem(line, 2) * TB, TB), TB)
                    out[2 * q, lax.div(line, 2), rows, columns] = e[:, :TB]
                    out[2 * q + 1, lax.div(line, 2), rows, columns] = e[:, TB:]
                else:
                    out[line, q, rows, :] = e
                total += jnp.sum(e.reshape(PB // 8, 8, 2 * TB), axis=0)
            total = jnp.sum(total, axis=0, keepdims=True)
            if side == 0:
                tx[x, side, pl.ds(8 * q + line, 1), :] = total[:, :TB]
                tx[x, side, pl.ds(8 * q + 4 + line, 1), :] = total[:, TB:]
            else:
                tx[x, side, pl.ds(4 * line + 2 * q, 1), :] = total[:, :TB]
                tx[x, side, pl.ds(4 * line + 2 * q + 1, 1), :] = total[:, TB:]
            return 0

        lax.fori_loop(0, 2, pair, 0)

    def forward(side):
        yield from projected(side)
        one, two = ("xy", "yx")[side]
        code = (cs, ct)[side]

        def send(i, j, to, at):
            ref = code.at[i, j] if side == 0 else code.at[j, i]
            return push(ref, ref, device(**{to: at}))

        first = place[one]
        at, ahead, behind, far = ring(two)
        sent = {d: send(first, at, one, lax.rem(first + d, 4)) for d in (2, 1, 3)}
        up, down, lines = [send(first, at, two, ahead)], [send(first, at, two, behind)], [first]
        yield
        for d in (1, 3, 2):
            sent[d].wait_recv()
            lines.append(lax.rem(first + 4 - d, 4))
            up.append(send(lines[-1], at, two, ahead))
            down.append(send(lines[-1], at, two, behind))
        yield
        on = []
        for copy, i in zip(up, lines):
            copy.wait_recv()
            on.append(send(i, behind, two, ahead))
        yield
        exponentials(side, at)
        exponentials(side, behind)
        for copy in down:
            copy.wait_recv()
        exponentials(side, ahead)
        yield
        for copy in on:
            copy.wait_recv()
        exponentials(side, far)

    def beside():
        for side, src, dst in features:
            got.setdefault(side, []).append(push(src, dst, device(core=other)))
        loads[2].wait()
        loads[3].wait()
        ps[z, core] = protos[0].T.astype(BF16)
        pt[z, core] = protos[1].T.astype(BF16)
        yield
        yield
        yield
        steps = [gather("z", lambda c, ref=ref: ref.at[c, core]) for ref in (ps, pt)]
        for step in steps:
            next(step)
        yield
        yield
        yield
        for copy in mine[0]:
            copy.wait_send()
        for a in range(2):
            for b in range(2):
                block = fx[0, a, :, pl.ds(768 * b, 768)].T
                w[a, b, :, :, :, 0:256] = block.reshape(4, 4, 48, 256)
        for step in steps:
            next(step)
        yield
        yt = (yf[0, core] + yr[0]).T
        n = jnp.sqrt(jnp.sum(yt * yt, axis=0, keepdims=True) + 1e-06)
        unit[...] = yt / n
        norm[0:1, :] = n
        for step in steps:
            run(step)
        swaps = [push(ref.at[:, core], ref.at[:, core], device(core=other)) for ref in (ps, pt)]
        yield
        for copy in swaps:
            copy.wait_recv()
        for b in range(NB):
            pn[:, b * PB : (b + 1) * PB] = ps[b // 2, b % 2].T

    run(forward(0), forward(1), beside())

    sent = [push(tx.at[x], tx.at[x], device(x=lax.rem(x + d, 4))) for d in (2, 1, 3)]
    for copy in sent:
        copy.wait_recv()
    ty[y] = tx[0] + tx[1] + tx[2] + tx[3]
    sent = [push(ty.at[y], ty.at[y], device(y=lax.rem(y + d, 4))) for d in (2, 1, 3)]
    for copy in sent:
        copy.wait_recv()
    tot[...] = (1.0 / tau_student) / (ty[0] + ty[1] + ty[2] + ty[3])

    def back(a, h):
        i = a * 2 + h
        inv_s = jnp.concatenate([tot[0, pl.ds(2 * i, 1), :], tot[0, pl.ds(2 * i + 1, 1), :]], 1)
        inv_t = jnp.concatenate([tot[1, pl.ds(2 * i, 1), :], tot[1, pl.ds(2 * i + 1, 1), :]], 1)
        columns = pl.ds(pl.multiple_of(i * 2 * TB, 2 * TB), 2 * TB)
        dh = jnp.zeros((256, 2 * TB), F32)
        for b in range(NB):
            rows = pl.ds(b * PB, PB)
            d = (es[a, h, rows, :] * inv_s - et[a, h, rows, :] * inv_t).astype(BF16)
            dz[rows, columns] = d
            dh += dot(pn[:, rows], d)
        dh = dh.astype(BF16)
        for d in range(2):
            columns = slice(d * TB, (d + 1) * TB)
            dh0[0, a, 2 * h + d] = dh[:128, columns]
            dh0[1, 2 * h + d, a] = dh[128:, columns]

    own, odd = lax.div(y, 2), lax.rem(y, 2)
    mate = 2 * own + 1 - odd
    across = [2 * (1 - own) + lax.rem(odd + e, 2) for e in range(2)]
    order = [(d, lax.rem(x + d, 4)) for d in (2, 1, 3, 0)]
    sent, sent_y = [[], []], []
    for n, h in enumerate((1 - own, own)):
        two = pl.ds(2 * h, 2)
        for i, (d, to) in enumerate(order):
            back(to, h)
            if d > 0:
                sent[n].append(push(dh0.at[0, to, two], dhr0.at[0, i, two], device(x=to)))
            for slot, to_y in ((1, across[0]), (2, across[1])) if n == 0 else ((0, mate),):
                sent_y.append(push(dh0.at[1, to_y, to], dhr0.at[1, slot, to], device(y=to_y)))

    passed = [[], []]

    def dh_rows(n):
        for copy in sent[n]:
            copy.wait_recv()
        for slot, to in ((1, across[0]), (2, across[1])) if n == 0 else ((0, mate), (None, y)):
            total = dh0[0, x, to].astype(F32)
            for i in range(3):
                total += dhr0[0, i, to].astype(F32)
            dh1[0, to] = total
            if slot is not None:
                passed[0].append(push(dh1.at[0, to], dhr1.at[0, slot], device(y=to)))

    def dh_columns(i):
        d, to = order[i]
        for at in (2 * i, 2 * i + 1, 8 + i):
            sent_y[at].wait_recv()
        total = dh0[1, y, to].astype(F32)
        for slot in range(3):
            total += dhr0[1, slot, to].astype(F32)
        dh1[1, to] = total
        if d > 0:
            passed[1].append(push(dh1.at[1, to], dhr1.at[1, i], device(x=to)))

    def proto_grad():
        def grad(block):
            rows = pl.ds(pl.multiple_of(block * PB, PB), PB)
            return dot(dz[rows, :], cs[...].reshape(NT, 256))

        def theirs(i, _):
            es[0, 0, pl.ds(pl.multiple_of(i * PB, PB), PB), :] = grad(i * 2 + other)
            return 0

        def ours(i, _):
            es[0, 1, pl.ds(pl.multiple_of(i * PB, PB), PB), :] = grad(i * 2 + core)
            return 0

        lax.fori_loop(0, 4, theirs, 0)
        swap = push(es.at[0, 0, pl.ds(0, 4 * PB), :], grecv, device(core=other))
        yield
        lax.fori_loop(0, 4, ours, 0)
        swap.wait_recv()
        gz[...] = (es[0, 1, : 4 * PB, :] + grecv[...]).astype(BF16).reshape(4, PB, 256)

        def last(v):
            g_proto[...] = v.T
            stores.append(load(g_proto, g_proto_out, 8))

        yield from scatter("z", gz, gzr, last)

    stores = []
    proto_steps = proto_grad()
    next(proto_steps)
    dh_rows(0)
    dh_columns(0)
    dh_columns(1)
    dh_rows(1)
    dh_columns(2)
    dh_columns(3)
    next(proto_steps)
    for k in range(2):
        for copy in passed[k]:
            copy.wait_recv()
        dht[k] = dh1[k, (y, x)[k]] + dhr1[k, 0] + dhr1[k, 1] + dhr1[k, 2]

    u = unit[...]
    dhv = jnp.concatenate([dht[0], dht[1]], axis=0)
    dyt = (dhv - u * jnp.sum(u * dhv, axis=0, keepdims=True)) / norm[0:1, :]
    dy[core] = dyt.astype(BF16)
    swap = push(dy.at[core], dy.at[core], device(core=other))
    swap.wait_recv()

    dyb = jnp.concatenate([dy[0], dy[1]], axis=1)
    for a in range(2):
        for b in range(2):
            c = b * 2 + a
            g = dot(w[a, b, :, :, :, 0:256].reshape(768, 256), dyb, ((1,), (1,))).astype(BF16)
            g = g.reshape(4, 4, 48, 256)
            for i in range(4):
                for j in range(4):
                    b0[0, i, j, c] = g[i, j, 0:16]
                    b0[1, j, c, i] = g[i, j, 16:32]
                    b0[2, c, i, j] = g[i, j, 32:48]

    def bot_scatter(k):
        one, two, three = ("xyz", "yzx", "zxy")[k]
        at, next_at = place[one], place[two]
        lines = [(d, lax.rem(next_at + d, 4)) for d in (2, 1, 3, 0)]
        first, second = [], []
        for _, j in lines:
            for i, d in enumerate((2, 1, 3)):
                to = lax.rem(at + d, 4)
                first.append(push(b0.at[k, to, j], br0.at[k, i, j], device(**{one: to})))
        yield
        for n, (d, j) in enumerate(lines):
            total = b0[k, at, j].astype(F32)
            for i in range(3):
                first[3 * n + i].wait_recv()
                total += br0[k, i, j].astype(F32)
            b1[k, j] = total
            if d > 0:
                second.append(push(b1.at[k, j], br1.at[k, n], device(**{two: j})))
            yield
        total = b1[k, next_at]
        for i, copy in enumerate(second):
            copy.wait_recv()
            total += br1[k, i]
        b2[k] = total

        def last(v):
            g_bot[16 * k : 16 * (k + 1), :] = v

        yield from scatter(three, b2.at[k], br2.at[k], last)

    run(*(bot_scatter(k) for k in range(3)), proto_steps)
    stores.append(load(g_bot, g_bot_out, 9))
    for copy in copies:
        if not any(copy is one for one in mine[0]):
            copy.wait_send()
    for copy in stores:
        copy.wait()


def gradients(feat_s, feat_t, bot_s, bot_t, proto_s, proto_t):
    vmem = pltpu.VMEM
    return pl.pallas_call(
        kernel,
        out_shape=(
            jax.ShapeDtypeStruct((48, 256), F32),
            jax.ShapeDtypeStruct((256, PB), F32),
        ),
        in_specs=[pl.BlockSpec(memory_space=pl.ANY)] * 6,
        out_specs=(pl.BlockSpec(memory_space=pl.ANY),) * 2,
        scratch_shapes=[
            vmem((2, 48, 256), F32),
            vmem((2, 256, PB), F32),
            vmem((48, 256), F32),
            vmem((256, PB), F32),
            vmem((2, 2, 4, 4, 48, 512), BF16),
            vmem((2, 2, 2 * TB, 1536), BF16),
            vmem((2, 2, TB, 256), F32),
            vmem((2, TB, 256), F32),
            vmem((256, TB), F32),
            vmem((8, TB), F32),
            vmem((4, 4, TB, 256), BF16),
            vmem((4, 4, TB, 256), BF16),
            vmem((4, 2, PB, 256), BF16),
            vmem((4, 2, PB, 256), BF16),
            vmem((256, NP), BF16),
            vmem((4, 2, NP, 2 * TB), F32),
            vmem((4, 2, NP, 2 * TB), F32),
            vmem((NP, NT), BF16),
            vmem((4, 2, 16, TB), F32),
            vmem((4, 2, 16, TB), F32),
            vmem((2, 16, TB), F32),
            vmem((2, 4, 4, 128, TB), BF16),
            vmem((2, 3, 4, 128, TB), BF16),
            vmem((2, 4, 128, TB), F32),
            vmem((2, 3, 128, TB), F32),
            vmem((2, 128, TB), F32),
            vmem((4 * PB, 256), F32),
            vmem((4, PB, 256), BF16),
            vmem((3, PB, 256), BF16),
            vmem((2, 256, TB), BF16),
            vmem((3, 4, 4, 4, 16, 256), BF16),
            vmem((3, 3, 4, 4, 16, 256), BF16),
            vmem((3, 4, 4, 16, 256), F32),
            vmem((3, 3, 4, 16, 256), F32),
            vmem((3, 4, 16, 256), F32),
            vmem((3, 3, 16, 256), F32),
            pltpu.SemaphoreType.DMA((SEMS,)),
            pltpu.SemaphoreType.DMA((SEMS,)),
            pltpu.SemaphoreType.DMA((10,)),
        ],
        compiler_params=pltpu.CompilerParams(
            collective_id=0, has_side_effects=True, vmem_limit_bytes=63 * 1024 * 1024
        ),
    )(feat_s, feat_t, bot_s, bot_t, proto_s, proto_t)


def per_device(feat_s, feat_t, bot_s, bot_m, bot_v, bot_t, proto_s, proto_m, proto_v, proto_t):
    g_bot, g_proto = gradients(feat_s, feat_t, bot_s, bot_t, proto_s, proto_t)
    return adamw(bot_s, bot_m, bot_v, g_bot, bot_t) + adamw(
        proto_s, proto_m, proto_v, g_proto, proto_t
    )


def solution(mesh):
    rows, columns = P(("dp", "fsdp"), None), P(None, ("fsdp", "dp"))
    return jax.shard_map(
        per_device,
        mesh=mesh,
        in_specs=(rows,) * 6 + (columns,) * 4,
        out_specs=(rows,) * 4 + (columns,) * 4,
        check_vma=False,
    )
```
